512 devices in a mesh: row: 16 (over z), col: 32 (over x, y, core).
Axes of the slice: x: 4, y: 4, z: 16, core: 2. Of those that a mesh axis runs over, the one named last changes fastest.
Arguments:
- pair: bfloat16 [1024, 1024, 128], P('row', 'col'), may hold values from -6 to 6
- pair_mask: int32 [1024, 1024], P('row', 'col'), may hold values from 0 to 1, as said below
- norm_gain: float32 [128], replicated, may hold values from 0.1 to 1.9
- norm_shift: float32 [128], replicated, may hold values from -3 to 3
- w_in: bfloat16 [128, 512], replicated, may hold values from -0.5 to 0.5
- out_gain: float32 [128], replicated, may hold values from 0.1 to 1.9
- out_shift: float32 [128], replicated, may hold values from -3 to 3
- w_out: bfloat16 [128, 128], replicated, may hold values from -0.5 to 0.5
- w_gate: bfloat16 [128, 128], replicated, may hold values from -0.5 to 0.5
Outputs:
- update: bfloat16 [1024, 1024, 128], P('row', 'col')
The draws below stay inside these ranges and needn't reach their ends.
Inputs may be any that keep to these rules, and one draw needn't show every extreme that they name: pair_mask[i, j] = valid[i] * valid[j] for a 0/1 vector valid over the 1024 tokens; the last tokens of the crop (one or more) are padding with valid 0, and some other tokens are invalid too.
All inputs are finite; a program needn't handle non-finite values.
Results may differ from the reference program's by a relative error of at most 0.0058.
Values may be sent and summed in bfloat16 or wider, within the bound.
A program may use at most 64 MiB of HBM per device.

```python
import jax
import jax.numpy as jnp
from jax import lax

N = 1024
C = 128


def draw_pair_mask(key, part):
    key = jax.random.fold_in(key, 11)
    pad_key, drop_key = jax.random.split(key)
    padding = jax.random.randint(pad_key, (), 1, N // 8 + 1)
    positions = jnp.arange(N, dtype=jnp.int32)
    inside = (positions < N - padding).astype(jnp.int32)
    kept = (jax.random.randint(drop_key, (N,), 0, 16) != 0).astype(jnp.int32)
    valid = inside * kept
    return (valid[:, None] * valid[None, :]).astype(jnp.int32)


def levels(stream_key, extent, cuts, low, high):
    factor_of = 1.0
    for dim, parts in cuts:
        heights = jax.random.uniform(jax.random.fold_in(jax.random.fold_in(stream_key, 6), dim), (parts,), jnp.float32, low / len(cuts), high / len(cuts))
        factor_of = factor_of * jnp.repeat(jnp.exp(heights), extent[dim] // parts).reshape((-1,) + (1,) * (len(extent) - 1 - dim))
    return factor_of


def bell_draw(rng, extent, width, bound, shards=(), kind=jnp.bfloat16):
    level = levels(rng, extent, shards, -0.22, 0.18) if shards else 1.0
    drawn = jax.random.normal(rng, extent, jnp.float32) * width * level
    return jnp.minimum(jnp.maximum(drawn, -bound), bound).astype(kind)


def setup_inputs(seed: int = 0) -> dict:
    streams_of = jax.random.split(jax.random.key(seed), 10)
    pair = bell_draw(streams_of[0], (N, N, C), 1.0, 6.0, ((0, 16), (1, 32)))
    pair_mask = draw_pair_mask(jax.random.fold_in(streams_of[9], 71), 0)
    norm_gain = jnp.clip(1.0 + 0.18 * jax.random.normal(streams_of[2], (C,), jnp.float32), 0.1, 1.9)
    norm_shift = bell_draw(streams_of[3], (C,), 0.5, 3.0, (), jnp.float32)
    w_in = bell_draw(streams_of[4], (C, 4 * C), C ** -0.5, 0.5)
    out_gain = jnp.clip(1.0 + 0.18 * jax.random.normal(streams_of[5], (C,), jnp.float32), 0.1, 1.9)
    out_shift = bell_draw(streams_of[6], (C,), 0.5, 3.0, (), jnp.float32)
    w_out = bell_draw(streams_of[7], (C, C), C ** -0.5, 0.5)
    w_gate = bell_draw(streams_of[8], (C, C), C ** -0.5, 0.5)
    return dict(pair=pair, pair_mask=pair_mask, norm_gain=norm_gain, norm_shift=norm_shift, w_in=w_in, out_gain=out_gain, out_shift=out_shift, w_out=w_out, w_gate=w_gate)


NORM_EPS = 1e-05

def layer_norm(values, gain_vec, shift_vec, norm_axis):
    centre = lax.optimization_barrier(jnp.mean(values, axis=norm_axis, keepdims=True))
    centred = values - centre
    second_moment = lax.optimization_barrier(jnp.mean(centred * centred, axis=norm_axis, keepdims=True))
    return centred * lax.rsqrt(second_moment + NORM_EPS) * gain_vec + shift_vec

def reference(pair, pair_mask, norm_gain, norm_shift, w_in, out_gain, out_shift, w_out, w_gate):
    normed = layer_norm(pair.astype(jnp.float32), norm_gain, norm_shift, -1).astype(jnp.bfloat16)
    normed_wide = normed.astype(jnp.float32)
    validity = pair_mask.astype(jnp.float32)
    w_parts = w_in.reshape(C, 4, C)

    def channel_product(channel_index):
        w_sel = lax.dynamic_index_in_dim(w_parts, channel_index, axis=2, keepdims=False).astype(jnp.float32)
        linear = jnp.einsum('ijc,ck->kij', normed_wide, w_sel, precision=lax.Precision.HIGHEST)
        left_panel = (validity * jax.nn.sigmoid(linear[1]) * linear[0]).astype(jnp.bfloat16)
        right_panel = (validity * jax.nn.sigmoid(linear[3]) * linear[2]).astype(jnp.bfloat16)
        total = jnp.dot(left_panel.astype(jnp.float32), right_panel.astype(jnp.float32).T, precision=lax.Precision.HIGHEST)
        return total.astype(jnp.bfloat16)
    products = lax.map(channel_product, jnp.arange(C, dtype=jnp.int32))

    def output_row(token_row):
        column_block = lax.dynamic_index_in_dim(products, token_row, axis=1, keepdims=False).astype(jnp.float32)
        normed_out = layer_norm(column_block, out_gain[:, None], out_shift[:, None], 0).astype(jnp.bfloat16)
        update = jnp.dot(normed_out.T, w_out, preferred_element_type=jnp.float32)
        gate_row = lax.dynamic_index_in_dim(normed, token_row, axis=0, keepdims=False)
        gate_value = jax.nn.sigmoid(jnp.dot(gate_row, w_gate, preferred_element_type=jnp.float32))
        return (gate_value * update).astype(jnp.bfloat16)
    return lax.map(output_row, jnp.arange(N, dtype=jnp.int32))
```

```python
import jax
import jax.numpy as jnp
from jax import lax
from jax.experimental import pallas as pl
from jax.experimental.pallas import tpu as pltpu
from jax.sharding import PartitionSpec as P

NORM_EPS = 1e-05
MESH = pl.DeviceIdType.MESH
ROWS, COLS = 16, 32
F32, BF16 = jnp.float32, jnp.bfloat16
BLOCK_ORDER = (0, 2, 1, 3)


def place(z, shift, lean):
    left = lax.rem(z - shift + 34 - lean, ROWS)
    right = lax.rem(z - shift + 22 - lean, ROWS)
    return left // 8, lax.rem(left, 8), right // 8, lax.rem(right, 8)


def plane_of(shift, left_half, right_half):
    corner = jnp.where(left_half == 0, right_half, 3 - right_half)
    return lax.rem(shift + 4 * corner, ROWS)


def body(
    pair, mask, norm_gain, norm_shift, w_in, out_gain, out_shift, w_out, w_gate,
    update,
    normed, wide_left, wide_right, w_turned, mask_rows, left_own, right_own,
    left_col, right_col, right_turned, left_in, right_in, tiles, tiles_in, gathered, wide_out, gate,
    gain_col, shift_col,
    send_left, send_right, recv_left, recv_right, send_z, recv_zl, recv_zr, send_t, recv_t, send_o, recv_o,
):
    z, d = lax.axis_index("row"), lax.axis_index("col")
    core = lax.rem(d, 2)

    barrier = pltpu.get_barrier_semaphore()

    def greet_row(s, carry):
        pl.semaphore_signal(barrier, inc=1, device_id=(lax.rem(z + s, ROWS), d), device_id_type=MESH)
        return carry

    def greet_col(s, carry):
        pl.semaphore_signal(barrier, inc=1, device_id=(z, lax.rem(d + s, COLS)), device_id_type=MESH)
        return carry

    lax.fori_loop(1, ROWS, greet_row, 0)
    lax.fori_loop(1, COLS, greet_col, 0)

    def norm_rows(t, carry):
        rows = pl.ds(pl.multiple_of(t * 256, 256), 256)
        x = pair[rows, :].astype(F32)
        centred = x - jnp.mean(x, axis=-1, keepdims=True)
        second = jnp.mean(centred * centred, axis=-1, keepdims=True)
        normed[rows, :] = centred * lax.rsqrt(second + NORM_EPS) * norm_gain[...] + norm_shift[...]
        return carry

    lax.fori_loop(0, 8, norm_rows, 0)
    w_turned[...] = w_in[...].astype(F32).T.astype(BF16)
    valid = mask[...].astype(F32)
    valid = jnp.concatenate([valid[16 * b : 16 * b + 16] for b in BLOCK_ORDER], axis=0).T
    mask_rows[...] = jnp.concatenate([valid[0:16], valid[16:32]], axis=1)

    def panel_step(kk, carry):
        pieces = [
            normed[pl.ds(b * 512 + k2 * 16 + kk, 16, stride=32), :] for k2 in range(2) for b in BLOCK_ORDER
        ]
        x = jnp.concatenate(pieces, axis=0).astype(BF16)
        linear = lax.dot_general(w_turned[...], x, (((1,), (1,)), ((), ())), preferred_element_type=F32)
        m = mask_rows[pl.ds(kk, 1), :]
        wide_left[pl.ds(kk, 128, stride=16), :] = m * jax.nn.sigmoid(linear[128:256]) * linear[0:128]
        wide_right[pl.ds(kk, 128, stride=16), :] = m * jax.nn.sigmoid(linear[384:512]) * linear[256:384]
        return carry

    lax.fori_loop(0, 16, panel_step, 0)
    left_own[...] = wide_left[...].astype(BF16).reshape(128, 16, 128)
    right_own[...] = wide_right[...].astype(BF16).reshape(128, 16, 128)

    pl.semaphore_wait(barrier, ROWS + COLS - 2)

    def spread(own, col, send, recv):
        def one(s, carry):
            to = lax.rem(d + s, COLS)
            pltpu.make_async_remote_copy(
                src_ref=own.at[pl.ds(4 * to, 4)], dst_ref=col.at[:, pl.ds(d * 16, 16), :],
                send_sem=send, recv_sem=recv, device_id=(z, to), device_id_type=MESH,
            ).start()
            return carry

        lax.fori_loop(1, COLS, one, 0)
        pltpu.make_async_copy(own.at[pl.ds(4 * d, 4)], col.at[:, pl.ds(d * 16, 16), :], recv).start()

    spread(left_own, left_col, send_left, recv_left)
    spread(right_own, right_col, send_right, recv_right)

    def left_copy(q, s):
        shift = q + 4 * core
        half, slot, _, _ = place(z, shift, core)
        to = plane_of(shift, half, s)
        return to, left_col.at[q], left_in.at[slot], send_z.at[2 * q + s], recv_zl

    def right_copy(q, s):
        shift = q + 4 * core
        _, _, half, slot = place(z, shift, core)
        to = plane_of(shift, s, half)
        return to, right_turned.at[q], right_in.at[slot], send_z.at[8 + 2 * q + s], recv_zr.at[slot]

    def launch(to, src, dst, send, recv):
        @pl.when(to != z)
        def _():
            pltpu.make_async_remote_copy(
                src_ref=src, dst_ref=dst, send_sem=send, recv_sem=recv, device_id=(to, d), device_id_type=MESH
            ).start()

        @pl.when(to == z)
        def _():
            pltpu.make_async_copy(src, dst, recv).start()

    def landed(to, src, dst, send, recv):
        @pl.when(to != z)
        def _():
            pltpu.make_async_remote_copy(
                src_ref=src, dst_ref=dst, send_sem=send, recv_sem=recv, device_id=(to, d), device_id_type=MESH
            ).wait_send()

    pltpu.make_async_copy(left_col, left_col, recv_left).wait()
    for q in range(4):
        for s in range(2):
            launch(*left_copy(q, s))
    pltpu.make_async_copy(right_col, right_col, recv_right).wait()
    for q in range(4):
        right_turned[q] = right_col[q].astype(F32).T.astype(BF16)
        for s in range(2):
            launch(*right_copy(q, s))

    def gate_rows(t, carry):
        rows = pl.ds(pl.multiple_of(t * 256, 256), 256)
        gate[rows, :] = jax.nn.sigmoid(
            jnp.dot(normed[rows, :].astype(BF16), w_gate[...], preferred_element_type=F32)
        )
        return carry

    lax.fori_loop(0, 8, gate_rows, 0)
    gain_col[...] = jnp.broadcast_to(out_gain[...], (128, 128)).T
    shift_col[...] = jnp.broadcast_to(out_shift[...], (128, 128)).T

    my_q = lax.rem(z, 4)
    my_shift = my_q + 4 * core
    corner = lax.rem(z - my_shift + 16, ROWS) // 4
    my_left = corner // 2
    my_right = jnp.where(my_left == 0, corner, 3 - corner)
    left_base = lax.rem(my_shift - 2 + core + 8 * my_left + 16, ROWS)
    right_base = lax.rem(my_shift + 10 + core + 8 * my_right, ROWS)

    lanes_low = lax.broadcasted_iota(jnp.int32, (32, 128), 1) < 64

    def tile_copy(slot, a):
        to = lax.rem(left_base + a, ROWS)
        block = lax.rem(right_base + slot, ROWS)
        return (
            to, tiles.at[slot, a], tiles_in.at[my_q, pl.ds(2 * block, 2)], send_t, recv_t
        )

    pltpu.make_async_copy(left_in, left_in, recv_zl).wait()

    def multiply(slot, carry):
        pltpu.make_async_copy(right_in.at[slot], right_in.at[slot], recv_zr.at[slot]).wait()
        for pair_index in range(4):
            both = jnp.concatenate([left_in[2 * pair_index], left_in[2 * pair_index + 1]], axis=1)
            grid = jnp.dot(right_in[slot], both, preferred_element_type=F32)
            for side in range(2):
                m = grid[:, 128 * side : 128 * side + 128]
                kept = jnp.where(lanes_low, m[0:32], m[96:128])
                moved = jnp.where(lanes_low, m[32:64], m[64:96])
                tile = (kept + pltpu.roll(moved, 64, axis=1)).astype(BF16)
                tiles[slot, 2 * pair_index + side] = tile.reshape(2, 16, 128)
        for a in range(8):
            launch(*tile_copy(slot, a))
        return carry

    lax.fori_loop(0, 8, multiply, 0)

    pltpu.make_async_copy(tiles_in, tiles_in, recv_t).wait()

    def return_one(s, carry):
        to = lax.rem(d + s, COLS)
        pltpu.make_async_remote_copy(
            src_ref=tiles_in.at[:, to], dst_ref=gathered.at[pl.ds(4 * d, 4)],
            send_sem=send_o, recv_sem=recv_o, device_id=(z, to), device_id_type=MESH,
        ).start()
        return carry

    lax.fori_loop(1, COLS, return_one, 0)
    pltpu.make_async_copy(tiles_in.at[:, d], gathered.at[pl.ds(4 * d, 4)], recv_o).start()

    pltpu.make_async_copy(left_own.at[pl.ds(0, 124)], left_own.at[pl.ds(0, 124)], send_left).wait()
    pltpu.make_async_copy(right_own.at[pl.ds(0, 124)], right_own.at[pl.ds(0, 124)], send_right).wait()
    for q in range(4):
        for s in range(2):
            landed(*left_copy(q, s))
            landed(*right_copy(q, s))

    def tile_left(slot, carry):
        for a in range(8):
            landed(*tile_copy(slot, a))
        return carry

    lax.fori_loop(0, 8, tile_left, 0)

    pltpu.make_async_copy(gathered, gathered, recv_o).wait()

    def total(t, carry):
        block = gathered[pl.ds(8 * t, 8)].astype(F32)
        return carry + jnp.sum(block, axis=0)

    centre = lax.fori_loop(0, 16, total, jnp.zeros((16, 128), F32)) * (1.0 / 128)

    def squares(t, carry):
        block = gathered[pl.ds(8 * t, 8)].astype(F32) - centre[None]
        return carry + jnp.sum(block * block, axis=0)

    second = lax.fori_loop(0, 16, squares, jnp.zeros((16, 128), F32)) * (1.0 / 128)
    scale = lax.rsqrt(second + NORM_EPS)

    def centre_rows(t, carry):
        block = (gathered[pl.ds(8 * t, 8)].astype(F32) - centre[None]) * scale[None]
        wide_out[pl.ds(pl.multiple_of(t * 128, 128), 128), :] = block.reshape(128, 128)
        return carry

    lax.fori_loop(0, 16, centre_rows, 0)

    def project(jj, carry):
        x = wide_out[pl.ds(jj, 128, stride=16), :] * gain_col[...] + shift_col[...]
        out = jnp.dot(x.T.astype(BF16), w_out[...], preferred_element_type=F32)
        for j2 in range(2):
            for s, b in enumerate(BLOCK_ORDER):
                rows = pl.ds(b * 512 + j2 * 16 + jj, 16, stride=32)
                gate[rows, :] = gate[rows, :] * out[64 * j2 + 16 * s : 64 * j2 + 16 * s + 16]
        return carry

    lax.fori_loop(0, 16, project, 0)
    update[...] = gate[...].astype(BF16)

    pltpu.make_async_copy(tiles_in.at[:, pl.ds(0, 31)], tiles_in.at[:, pl.ds(0, 31)], send_o).wait()


def on_device(pair, pair_mask, norm_gain, norm_shift, w_in, out_gain, out_shift, w_out, w_gate):
    vmem = pl.BlockSpec(memory_space=pltpu.VMEM)
    dma = pltpu.SemaphoreType.DMA
    out = pl.pallas_call(
        body,
        out_shape=jax.ShapeDtypeStruct((2048, 128), BF16),
        in_specs=[vmem] * 9,
        out_specs=vmem,
        scratch_shapes=[
            pltpu.VMEM((2048, 128), F32),
            pltpu.VMEM((2048, 128), F32),
            pltpu.VMEM((2048, 128), F32),
            pltpu.VMEM((512, 128), BF16),
            pltpu.VMEM((16, 128), F32),
            pltpu.VMEM((128, 16, 128), BF16),
            pltpu.VMEM((128, 16, 128), BF16),
            pltpu.VMEM((4, 512, 128), BF16),
            pltpu.VMEM((4, 512, 128), BF16),
            pltpu.VMEM((4, 128, 512), BF16),
            pltpu.VMEM((8, 512, 128), BF16),
            pltpu.VMEM((8, 128, 512), BF16),
            pltpu.VMEM((8, 8, 2, 16, 128), BF16),
            pltpu.VMEM((4, 32, 16, 128), BF16),
            pltpu.VMEM((128, 16, 128), BF16),
            pltpu.VMEM((2048, 128), F32),
            pltpu.VMEM((2048, 128), F32),
            pltpu.VMEM((128, 128), F32),
            pltpu.VMEM((128, 128), F32),
            dma, dma, dma, dma,
            dma((16,)), dma, dma((8,)),
            dma, dma, dma, dma,
        ],
        compiler_params=pltpu.CompilerParams(
            collective_id=0, has_side_effects=True, vmem_limit_bytes=40 << 20
        ),
    )(
        pair.reshape(2048, 128), pair_mask, norm_gain.reshape(1, 128), norm_shift.reshape(1, 128), w_in,
        out_gain.reshape(1, 128), out_shift.reshape(1, 128), w_out, w_gate,
    )
    return out.reshape(64, 32, 128)


def solution(mesh):
    in_specs = (P("row", "col", None), P("row", "col"), P(), P(), P(), P(), P(), P(), P())
    out_specs = P("row", "col", None)
    return jax.shard_map(on_device, mesh=mesh, in_specs=in_specs, out_specs=out_specs, check_vma=False)
```

```python
import jax
import jax.numpy as jnp
from jax import lax
from jax.experimental import pallas as pl
from jax.experimental.pallas import tpu as pltpu
from jax.sharding import PartitionSpec as P

NORM_EPS = 1e-05
MESH = pl.DeviceIdType.MESH
ROWS, COLS = 16, 32
F32, BF16 = jnp.float32, jnp.bfloat16
BLOCK_ORDER = (0, 2, 1, 3)


def place(z, shift, lean):
    left = lax.rem(z - shift + 34 - lean, ROWS)
    right = lax.rem(z - shift + 22 - lean, ROWS)
    return left // 8, lax.rem(left, 8), right // 8, lax.rem(right, 8)


def plane_of(shift, left_half, right_half):
    corner = jnp.where(left_half == 0, right_half, 3 - right_half)
    return lax.rem(shift + 4 * corner, ROWS)


def body(
    pair_hbm, mask_hbm, norm_gain_hbm, norm_shift_hbm, w_in_hbm, out_gain_hbm, out_shift_hbm, w_out_hbm, w_gate_hbm,
    update,
    pair, mask, norm_gain, norm_shift, w_in, out_gain, out_shift, w_out, w_gate, load,
    normed, wide_left, wide_right, w_turned, mask_rows, left_own, right_own,
    left_col, right_col, right_turned, left_in, right_in, tiles, tiles_in, gathered, wide_out, gate,
    gain_col, shift_col,
    send_left, send_right, recv_left, recv_right, send_z, recv_zl, recv_zr, send_t, recv_t, send_o, recv_o,
):
    z, d = lax.axis_index("row"), lax.axis_index("col")
    core = lax.rem(d, 2)

    operands = (
        (pair_hbm, pair), (mask_hbm, mask), (norm_gain_hbm, norm_gain), (norm_shift_hbm, norm_shift), (w_in_hbm, w_in),
        (out_gain_hbm, out_gain), (out_shift_hbm, out_shift), (w_out_hbm, w_out), (w_gate_hbm, w_gate),
    )
    loads = [pltpu.make_async_copy(src, dst, load.at[n]) for n, (src, dst) in enumerate(operands)]
    for copy in loads:
        copy.start()

    barrier = pltpu.get_barrier_semaphore()

    def greet_row(s, carry):
        pl.semaphore_signal(barrier, inc=1, device_id=(lax.rem(z + s, ROWS), d), device_id_type=MESH)
        return carry

    def greet_col(s, carry):
        pl.semaphore_signal(barrier, inc=1, device_id=(z, lax.rem(d + s, COLS)), device_id_type=MESH)
        return carry

    lax.fori_loop(1, ROWS, greet_row, 0)
    lax.fori_loop(1, COLS, greet_col, 0)

    for copy in loads:
        copy.wait()

    def norm_rows(t, carry):
        rows = pl.ds(pl.multiple_of(t * 256, 256), 256)
        x = pair[rows, :].astype(F32)
        centred = x - jnp.mean(x, axis=-1, keepdims=True)
        second = jnp.mean(centred * centred, axis=-1, keepdims=True)
        normed[rows, :] = centred * lax.rsqrt(second + NORM_EPS) * norm_gain[...] + norm_shift[...]
        return carry

    lax.fori_loop(0, 8, norm_rows, 0)
    w_turned[...] = w_in[...].astype(F32).T.astype(BF16)
    valid = mask[...].astype(F32)
    valid = jnp.concatenate([valid.T[16 * b : 16 * b + 16] for b in BLOCK_ORDER], axis=0).T
    mask_rows[...] = jnp.concatenate([valid[0:16], valid[16:32]], axis=1)

    def panel_step(kk, carry):
        pieces = [
            normed[pl.ds(b * 512 + k2 * 16 + kk, 16, stride=32), :] for k2 in range(2) for b in BLOCK_ORDER
        ]
        x = jnp.concatenate(pieces, axis=0).astype(BF16)
        linear = lax.dot_general(w_turned[...], x, (((1,), (1,)), ((), ())), preferred_element_type=F32)
        m = mask_rows[pl.ds(kk, 1), :]
        wide_left[pl.ds(kk, 128, stride=16), :] = m * jax.nn.sigmoid(linear[128:256]) * linear[0:128]
        wide_right[pl.ds(kk, 128, stride=16), :] = m * jax.nn.sigmoid(linear[384:512]) * linear[256:384]
        return carry

    lax.fori_loop(0, 16, panel_step, 0)
    left_own[...] = wide_left[...].astype(BF16).reshape(128, 16, 128)
    right_own[...] = wide_right[...].astype(BF16).reshape(128, 16, 128)

    pl.semaphore_wait(barrier, ROWS + COLS - 2)

    panels = ((left_own, left_col, send_left, recv_left), (right_own, right_col, send_right, recv_right))

    def spread(which, i):
        own, col, send, recv = panels[which]
        q = lax.rem(z + i, 4)

        def one(s, carry):
            to = lax.rem(d + s, COLS)
            pltpu.make_async_remote_copy(
                src_ref=own.at[4 * to + q], dst_ref=col.at[q, pl.ds(d * 16, 16), :],
                send_sem=send, recv_sem=recv.at[i], device_id=(z, to), device_id_type=MESH,
            ).start()
            return carry

        lax.fori_loop(1, COLS, one, 0)
        pltpu.make_async_copy(own.at[4 * d + q], col.at[q, pl.ds(d * 16, 16), :], recv.at[i]).start()

    def spread_done(which, i):
        _, col, _, recv = panels[which]
        pltpu.make_async_copy(col.at[0], col.at[0], recv.at[i]).wait()

    def left_copy(i, s):
        q = lax.rem(z + i, 4)
        shift = q + 4 * core
        half, slot, _, _ = place(z, shift, core)
        to = plane_of(shift, half, s)
        return to, left_col.at[q], left_in.at[2 * i + slot // 4], send_z.at[2 * i + s], recv_zl

    def right_copy(i, s):
        q = lax.rem(z + i, 4)
        shift = q + 4 * core
        _, _, half, slot = place(z, shift, core)
        to = plane_of(shift, s, half)
        return to, right_turned.at[q], right_in.at[2 * i + slot // 4], send_z.at[8 + 2 * i + s], recv_zr.at[i]

    def launch(to, src, dst, send, recv):
        @pl.when(to != z)
        def _():
            pltpu.make_async_remote_copy(
                src_ref=src, dst_ref=dst, send_sem=send, recv_sem=recv, device_id=(to, d), device_id_type=MESH
            ).start()

        @pl.when(to == z)
        def _():
            pltpu.make_async_copy(src, dst, recv).start()

    def landed(to, src, dst, send, recv):
        @pl.when(to != z)
        def _():
            pltpu.make_async_remote_copy(
                src_ref=src, dst_ref=dst, send_sem=send, recv_sem=recv, device_id=(to, d), device_id_type=MESH
            ).wait_send()

    spread(0, 0)
    spread(0, 1)
    for chunk in range(8):
        which, i = chunk // 4, chunk % 4
        spread_done(which, i)
        if which == 1:
            q = lax.rem(z + i, 4)
            right_turned[q] = right_col[q].astype(F32).T.astype(BF16)
        for s in range(2):
            launch(*(right_copy(i, s) if which else left_copy(i, s)))
        if chunk + 2 < 8:
            spread((chunk + 2) // 4, (chunk + 2) % 4)

    def gate_rows(t, carry):
        rows = pl.ds(pl.multiple_of(t * 256, 256), 256)
        gate[rows, :] = jax.nn.sigmoid(
            jnp.dot(normed[rows, :].astype(BF16), w_gate[...], preferred_element_type=F32)
        )
        return carry

    lax.fori_loop(0, 8, gate_rows, 0)
    gain_col[...] = jnp.broadcast_to(out_gain[...], (128, 128)).T
    shift_col[...] = jnp.broadcast_to(out_shift[...], (128, 128)).T

    my_q = lax.rem(z, 4)
    my_shift = my_q + 4 * core
    corner = lax.rem(z - my_shift + 16, ROWS) // 4
    my_left = corner // 2
    my_right = jnp.where(my_left == 0, corner, 3 - corner)
    left_base = lax.rem(my_shift - 2 + core + 8 * my_left + 16, ROWS)
    right_base = lax.rem(my_shift + 10 + core + 8 * my_right, ROWS)

    lanes_low = lax.broadcasted_iota(jnp.int32, (32, 128), 1) < 64

    def tile_copy(i, h, a):
        to = lax.rem(left_base + lax.rem(10 - core - a // 2, 4) + 4 * (a % 2), ROWS)
        block = lax.rem(right_base + lax.rem(10 - core - i, 4) + 4 * h, ROWS)
        return (
            to, tiles.at[2 * i + h, a], tiles_in.at[my_q, pl.ds(2 * block, 2)], send_t, recv_t.at[i]
        )

    def multiply(i, h):
        right = right_in[2 * i + h]
        for pair_index in range(4):
            both = jnp.concatenate([left_in[2 * pair_index], left_in[2 * pair_index + 1]], axis=1)
            grid = jnp.dot(right, both, preferred_element_type=F32)
            for side in range(2):
                m = grid[:, 128 * side : 128 * side + 128]
                kept = jnp.where(lanes_low, m[0:32], m[96:128])
                moved = jnp.where(lanes_low, m[32:64], m[64:96])
                tile = (kept + pltpu.roll(moved, 64, axis=1)).astype(BF16)
                tiles[2 * i + h, 2 * pair_index + side] = tile.reshape(2, 16, 128)
                launch(*tile_copy(i, h, 2 * pair_index + side))

    def hand_on(i):
        pltpu.make_async_copy(tiles_in.at[0], tiles_in.at[0], recv_t.at[i]).wait()

        def one(s, carry):
            to = lax.rem(d + s, COLS)
            q = lax.rem(to // 2 + i, 4)
            pltpu.make_async_remote_copy(
                src_ref=tiles_in.at[q, to], dst_ref=gathered.at[4 * d + q],
                send_sem=send_o, recv_sem=recv_o, device_id=(z, to), device_id_type=MESH,
            ).start()
            return carry

        lax.fori_loop(1, COLS, one, 0)
        q = lax.rem(d // 2 + i, 4)
        pltpu.make_async_copy(tiles_in.at[q, d], gathered.at[4 * d + q], recv_o).start()

    pltpu.make_async_copy(left_in, left_in, recv_zl).wait()

    def step(i, carry):
        pltpu.make_async_copy(right_in.at[pl.ds(0, 2)], right_in.at[pl.ds(0, 2)], recv_zr.at[i]).wait()

        def half(h, carry):
            multiply(i, h)
            return carry

        lax.fori_loop(0, 2, half, 0)

        @pl.when(i > 0)
        def _():
            hand_on(i - 1)

        return carry

    lax.fori_loop(0, 4, step, 0)
    hand_on(3)

    pltpu.make_async_copy(left_own.at[pl.ds(0, 124)], left_own.at[pl.ds(0, 124)], send_left).wait()
    pltpu.make_async_copy(right_own.at[pl.ds(0, 124)], right_own.at[pl.ds(0, 124)], send_right).wait()
    for i in range(4):
        for s in range(2):
            landed(*left_copy(i, s))
            landed(*right_copy(i, s))

    def tile_left(i, carry):
        for h in range(2):
            for a in range(8):
                landed(*tile_copy(i, h, a))
        return carry

    lax.fori_loop(0, 4, tile_left, 0)

    pltpu.make_async_copy(gathered, gathered, recv_o).wait()

    def total(t, carry):
        block = gathered[pl.ds(8 * t, 8)].astype(F32)
        return carry + jnp.sum(block, axis=0)

    centre = lax.fori_loop(0, 16, total, jnp.zeros((16, 128), F32)) * (1.0 / 128)

    def squares(t, carry):
        block = gathered[pl.ds(8 * t, 8)].astype(F32) - centre[None]
        return carry + jnp.sum(block * block, axis=0)

    second = lax.fori_loop(0, 16, squares, jnp.zeros((16, 128), F32)) * (1.0 / 128)
    scale = lax.rsqrt(second + NORM_EPS)

    def centre_rows(t, carry):
        block = (gathered[pl.ds(8 * t, 8)].astype(F32) - centre[None]) * scale[None]
        wide_out[pl.ds(pl.multiple_of(t * 128, 128), 128), :] = block.reshape(128, 128)
        return carry

    lax.fori_loop(0, 16, centre_rows, 0)

    def project(jj, carry):
        x = wide_out[pl.ds(jj, 128, stride=16), :] * gain_col[...] + shift_col[...]
        out = jnp.dot(x.T.astype(BF16), w_out[...], preferred_element_type=F32)
        for j2 in range(2):
            for s, b in enumerate(BLOCK_ORDER):
                rows = pl.ds(b * 512 + j2 * 16 + jj, 16, stride=32)
                gate[rows, :] = gate[rows, :] * out[64 * j2 + 16 * s : 64 * j2 + 16 * s + 16]
        return carry

    lax.fori_loop(0, 16, project, 0)
    update[...] = gate[...].astype(BF16)

    pltpu.make_async_copy(tiles_in.at[:, pl.ds(0, 31)], tiles_in.at[:, pl.ds(0, 31)], send_o).wait()


def on_device(pair, pair_mask, norm_gain, norm_shift, w_in, out_gain, out_shift, w_out, w_gate):
    vmem = pl.BlockSpec(memory_space=pltpu.VMEM)
    dma = pltpu.SemaphoreType.DMA
    out = pl.pallas_call(
        body,
        out_shape=jax.ShapeDtypeStruct((2048, 128), BF16),
        in_specs=[pl.BlockSpec(memory_space=pl.ANY)] * 9,
        out_specs=vmem,
        scratch_shapes=[
            pltpu.VMEM((2048, 128), BF16),
            pltpu.VMEM((32, 64), jnp.int32),
            pltpu.VMEM((1, 128), F32),
            pltpu.VMEM((1, 128), F32),
            pltpu.VMEM((128, 512), BF16),
            pltpu.VMEM((1, 128), F32),
            pltpu.VMEM((1, 128), F32),
            pltpu.VMEM((128, 128), BF16),
            pltpu.VMEM((128, 128), BF16),
            dma((9,)),
            pltpu.VMEM((2048, 128), F32),
            pltpu.VMEM((2048, 128), F32),
            pltpu.VMEM((2048, 128), F32),
            pltpu.VMEM((512, 128), BF16),
            pltpu.VMEM((16, 128), F32),
            pltpu.VMEM((128, 16, 128), BF16),
            pltpu.VMEM((128, 16, 128), BF16),
            pltpu.VMEM((4, 512, 128), BF16),
            pltpu.VMEM((4, 512, 128), BF16),
            pltpu.VMEM((4, 128, 512), BF16),
            pltpu.VMEM((8, 512, 128), BF16),
            pltpu.VMEM((8, 128, 512), BF16),
            pltpu.VMEM((8, 8, 2, 16, 128), BF16),
            pltpu.VMEM((4, 32, 16, 128), BF16),
            pltpu.VMEM((128, 16, 128), BF16),
            pltpu.VMEM((2048, 128), F32),
            pltpu.VMEM((2048, 128), F32),
            pltpu.VMEM((128, 128), F32),
            pltpu.VMEM((128, 128), F32),
            dma, dma, dma((4,)), dma((4,)),
            dma((16,)), dma, dma((4,)),
            dma, dma((4,)), dma, dma,
        ],
        compiler_params=pltpu.CompilerParams(
            collective_id=0, has_side_effects=True, vmem_limit_bytes=56 << 20
        ),
    )(
        pair.reshape(2048, 128), pair_mask.T, norm_gain.reshape(1, 128), norm_shift.reshape(1, 128), w_in,
        out_gain.reshape(1, 128), out_shift.reshape(1, 128), w_out, w_gate,
    )
    return out.reshape(64, 32, 128)


def solution(mesh):
    in_specs = (P("row", "col", None), P("row", "col"), P(), P(), P(), P(), P(), P(), P())
    out_specs = P("row", "col", None)
    return jax.shard_map(on_device, mesh=mesh, in_specs=in_specs, out_specs=out_specs, check_vma=False)
```

```python
import jax
import jax.numpy as jnp
from jax import lax
from jax.experimental import pallas as pl
from jax.experimental.pallas import tpu as pltpu
from jax.sharding import PartitionSpec as P

NORM_EPS = 1e-05
MESH = pl.DeviceIdType.MESH
ROWS, COLS = 16, 32
REACH = 6
F32, BF16 = jnp.float32, jnp.bfloat16
BLOCK_ORDER = (0, 2, 1, 3)


def place(z, shift, lean):
    left = lax.rem(z - shift + 34 - lean, ROWS)
    right = lax.rem(z - shift + 22 - lean, ROWS)
    return left // 8, lax.rem(left, 8), right // 8, lax.rem(right, 8)


def plane_of(shift, left_half, right_half):
    corner = jnp.where(left_half == 0, right_half, 3 - right_half)
    return lax.rem(shift + 4 * corner, ROWS)


def body(
    pair_hbm, mask_hbm, norm_gain_hbm, norm_shift_hbm, w_in_hbm, out_gain_hbm, out_shift_hbm, w_out_hbm, w_gate_hbm,
    update,
    pair, mask, norm_gain, norm_shift, w_in, out_gain, out_shift, w_out, w_gate, load,
    normed, wide_left, wide_right, w_turned, mask_rows, own, left_early,
    col, right_turned, left_in, right_in, tiles, gathered, wide_out, gate,
    gain_col, shift_col,
    send_c, recv_c, send_z, recv_zl, recv_zr, send_t, recv_o, send_e, recv_e, send_f,
):
    z, d = lax.axis_index("row"), lax.axis_index("col")
    core = lax.rem(d, 2)

    operands = (
        (pair_hbm, pair), (mask_hbm, mask), (norm_gain_hbm, norm_gain), (norm_shift_hbm, norm_shift), (w_in_hbm, w_in),
        (out_gain_hbm, out_gain), (out_shift_hbm, out_shift), (w_out_hbm, w_out), (w_gate_hbm, w_gate),
    )
    loads = [pltpu.make_async_copy(src, dst, load.at[n]) for n, (src, dst) in enumerate(operands)]
    for copy in loads:
        copy.start()

    barrier = pltpu.get_barrier_semaphore()

    def greet_row(s, carry):
        pl.semaphore_signal(barrier, inc=1, device_id=(lax.rem(z + s, ROWS), d), device_id_type=MESH)
        return carry

    def greet_col(s, carry):
        pl.semaphore_signal(barrier, inc=1, device_id=(z, lax.rem(d + s, COLS)), device_id_type=MESH)
        return carry

    lax.fori_loop(1, REACH + 1, greet_row, 0)
    lax.fori_loop(ROWS - REACH, ROWS, greet_row, 0)
    lax.fori_loop(1, COLS, greet_col, 0)

    for copy in loads:
        copy.wait()

    def norm_rows(t, carry):
        rows = pl.ds(pl.multiple_of(t * 256, 256), 256)
        x = pair[rows, :].astype(F32)
        centred = x - jnp.mean(x, axis=-1, keepdims=True)
        second = jnp.mean(centred * centred, axis=-1, keepdims=True)
        normed[rows, :] = centred * lax.rsqrt(second + NORM_EPS) * norm_gain[...] + norm_shift[...]
        return carry

    lax.fori_loop(0, 8, norm_rows, 0)
    w_turned[...] = w_in[...].astype(F32).T.astype(BF16)
    valid = mask[...].astype(F32)
    valid = jnp.concatenate([valid.T[16 * b : 16 * b + 16] for b in BLOCK_ORDER], axis=0).T
    mask_rows[...] = jnp.concatenate([valid[0:16], valid[16:32]], axis=1)

    def panel_step(kk, carry):
        pieces = [
            normed[pl.ds(b * 512 + k2 * 16 + kk, 16, stride=32), :] for k2 in range(2) for b in BLOCK_ORDER
        ]
        x = jnp.concatenate(pieces, axis=0).astype(BF16)
        linear = lax.dot_general(w_turned[...], x, (((1,), (1,)), ((), ())), preferred_element_type=F32)
        m = mask_rows[pl.ds(kk, 1), :]
        wide_left[pl.ds(kk, 128, stride=16), :] = m * jax.nn.sigmoid(linear[128:256]) * linear[0:128]
        wide_right[pl.ds(kk, 128, stride=16), :] = m * jax.nn.sigmoid(linear[384:512]) * linear[256:384]
        return carry

    lax.fori_loop(0, 16, panel_step, 0)
    own[:, :, :, 0] = wide_left[...].astype(BF16).reshape(16, 2, 4, 16, 128)
    own[:, :, :, 1] = wide_right[...].astype(BF16).reshape(16, 2, 4, 16, 128)

    pl.semaphore_wait(barrier, 2 * REACH + COLS - 1)

    def rank_at(turn):
        if isinstance(turn, int) and turn in (0, 3):
            return (0, 0, 0, 2)[turn]
        late = jnp.where(turn == 3, 2, jnp.where(turn == 1, 1 + 2 * core, 3 - 2 * core))
        return jnp.where(turn == 0, 0, late)

    def spread(turn):
        i = rank_at(turn)
        q = lax.rem(z + i, 4)
        side = 1 if turn == 0 else slice(None)
        there = col.at[q, side, pl.ds(d * 16, 16), :]

        def one(s, carry):
            to = lax.rem(d + s, COLS)
            pltpu.make_async_remote_copy(
                src_ref=own.at[to // 2, to % 2, q, side], dst_ref=there,
                send_sem=send_c, recv_sem=recv_c.at[i], device_id=(z, to), device_id_type=MESH,
            ).start()
            return carry

        lax.fori_loop(1, COLS, one, 0)
        pltpu.make_async_copy(own.at[d // 2, core, q, side], there, recv_c.at[i]).start()

    def spread_done(turn):
        got = col.at[0, 0] if turn == 0 else col.at[0]
        pltpu.make_async_copy(got, got, recv_c.at[rank_at(turn)]).wait()

    def left_copy(turn, s):
        i = rank_at(turn)
        q = lax.rem(z + i, 4)
        shift = q + 4 * core
        half, slot, _, _ = place(z, shift, core)
        to = plane_of(shift, half, s)
        send = send_z.at[2 * turn + s]
        return to, col.at[q, 0], left_in.at[2 * i + slot // 4], send, recv_zl

    def right_copy(turn, s):
        i = rank_at(turn)
        q = lax.rem(z + i, 4)
        shift = q + 4 * core
        _, _, half, slot = place(z, shift, core)
        to = plane_of(shift, s, half)
        send = send_z.at[8 + 2 * turn + s]
        return to, right_turned.at[q], right_in.at[2 * i + slot // 4], send, recv_zr.at[i]

    def launch(to, src, dst, send, recv):
        @pl.when(to != z)
        def _():
            pltpu.make_async_remote_copy(
                src_ref=src, dst_ref=dst, send_sem=send, recv_sem=recv, device_id=(to, d), device_id_type=MESH
            ).start()

        @pl.when(to == z)
        def _():
            pltpu.make_async_copy(src, dst, recv).start()

    def landed(to, src, dst, send, recv):
        @pl.when(to != z)
        def _():
            pltpu.make_async_remote_copy(
                src_ref=src, dst_ref=dst, send_sem=send, recv_sem=recv, device_id=(to, d), device_id_type=MESH
            ).wait_send()

    def early_copy(c, s):
        q = lax.rem(z, 4)
        half, slot, _, _ = place(z, q + 4 * c, c)
        to = plane_of(q + 4 * c, half, s)
        return to, own.at[:, c, q, 0], left_early.at[slot // 4, c], send_f.at[2 * c + s], recv_e

    def early_out():
        pltpu.make_async_copy(left_early, left_early, recv_e).wait()

        def one(s, carry):
            to = lax.rem(d + s, COLS)
            pltpu.make_async_remote_copy(
                src_ref=left_early.at[:, to % 2, to // 2], dst_ref=left_in.at[pl.ds(0, 2), pl.ds(d * 16, 16), :],
                send_sem=send_e, recv_sem=recv_zl, device_id=(z, to), device_id_type=MESH,
            ).start()
            return carry

        lax.fori_loop(1, COLS, one, 0)
        pltpu.make_async_copy(left_early.at[:, core, d // 2], left_in.at[pl.ds(0, 2), pl.ds(d * 16, 16), :], recv_zl).start()

    def send_lefts(turn):
        spread_done(turn)
        for s in range(2):
            launch(*left_copy(turn, s))

    def send_rights(turn):
        q = lax.rem(z + rank_at(turn), 4)
        right_turned[q] = col[q, 1].astype(F32).T.astype(BF16)
        for s in range(2):
            launch(*right_copy(turn, s))

    for s in range(2):
        for c in range(2):
            launch(*early_copy(c, s))
    spread(1)
    spread(2)
    send_lefts(1)
    spread(3)
    send_lefts(2)
    spread(0)
    send_lefts(3)
    early_out()
    for turn in (1, 2, 3):
        send_rights(turn)
    spread_done(0)
    send_rights(0)

    def gate_rows(t, carry):
        rows = pl.ds(pl.multiple_of(t * 256, 256), 256)
        gate[rows, :] = jax.nn.sigmoid(
            jnp.dot(normed[rows, :].astype(BF16), w_gate[...], preferred_element_type=F32)
        )
        return carry

    lax.fori_loop(0, 8, gate_rows, 0)
    gain_col[...] = jnp.broadcast_to(out_gain[...], (128, 128)).T
    shift_col[...] = jnp.broadcast_to(out_shift[...], (128, 128)).T

    my_q = lax.rem(z, 4)
    my_shift = my_q + 4 * core
    corner = lax.rem(z - my_shift + 16, ROWS) // 4
    my_left = corner // 2
    my_right = jnp.where(my_left == 0, corner, 3 - corner)
    left_base = lax.rem(my_shift - 2 + core + 8 * my_left + 16, ROWS)
    right_base = lax.rem(my_shift + 10 + core + 8 * my_right, ROWS)

    lanes_low = lax.broadcasted_iota(jnp.int32, (32, 128), 1) < 64

    def tile_send(i, h, a, half):
        row = lax.rem(left_base + lax.rem(10 - core - a // 2, 4) + 4 * (a % 2), ROWS)
        block = lax.rem(right_base + lax.rem(10 - core - i, 4) + 4 * h, ROWS)
        to = 2 * block + half
        src, dst = tiles.at[2 * i + h, a, half], gathered.at[4 * d + my_q]
        here = (row == z) & (to == d)

        @pl.when(jnp.logical_not(here))
        def _():
            pltpu.make_async_remote_copy(
                src_ref=src, dst_ref=dst, send_sem=send_t, recv_sem=recv_o, device_id=(row, to), device_id_type=MESH
            ).start()

        @pl.when(here)
        def _():
            pltpu.make_async_copy(src, dst, recv_o).start()

    def multiply(i, h):
        right = right_in[2 * i + h]
        for pair_index in range(4):
            both = jnp.concatenate([left_in[2 * pair_index], left_in[2 * pair_index + 1]], axis=1)
            grid = jnp.dot(right, both, preferred_element_type=F32)
            for side in range(2):
                m = grid[:, 128 * side : 128 * side + 128]
                kept = jnp.where(lanes_low, m[0:32], m[96:128])
                moved = jnp.where(lanes_low, m[32:64], m[64:96])
                tile = (kept + pltpu.roll(moved, 64, axis=1)).astype(BF16)
                a = 2 * pair_index + side
                tiles[2 * i + h, a] = tile.reshape(2, 16, 128)
                for half in range(2):
                    tile_send(i, h, a, half)

    pltpu.make_async_copy(left_in, left_in, recv_zl).wait()

    for turn in (1, 2, 3, 0):
        i = rank_at(turn)
        pltpu.make_async_copy(right_in.at[pl.ds(0, 2)], right_in.at[pl.ds(0, 2)], recv_zr.at[i]).wait()

        def half_rank(h, carry, i=i):
            multiply(i, h)
            return carry

        lax.fori_loop(0, 2, half_rank, 0)

    def gone(buffer, sem):
        pltpu.make_async_copy(buffer, buffer, sem).wait()

    gone(col.at[pl.ds(0, 3), :, pl.ds(0, 31 * 16)], send_c)
    gone(col.at[0, 0, pl.ds(0, 31 * 16)], send_c)
    gone(left_in.at[pl.ds(0, 2), pl.ds(0, 31 * 16)], send_e)
    for turn in range(4):
        for s in range(2):
            landed(*right_copy(turn, s))
            if turn:
                landed(*left_copy(turn, s))
    for s in range(2):
        for c in range(2):
            landed(*early_copy(c, s))
    gone(gathered.at[pl.ds(0, 127)], send_t)

    @pl.when(lax.rem(d // 2 - right_base + 2 * ROWS, ROWS) >= 8)
    def _():
        gone(gathered.at[0], send_t)

    pltpu.make_async_copy(gathered, gathered, recv_o).wait()

    def total(t, carry):
        block = gathered[pl.ds(8 * t, 8)].astype(F32)
        return carry + jnp.sum(block, axis=0)

    centre = lax.fori_loop(0, 16, total, jnp.zeros((16, 128), F32)) * (1.0 / 128)

    def squares(t, carry):
        block = gathered[pl.ds(8 * t, 8)].astype(F32) - centre[None]
        return carry + jnp.sum(block * block, axis=0)

    second = lax.fori_loop(0, 16, squares, jnp.zeros((16, 128), F32)) * (1.0 / 128)
    scale = lax.rsqrt(second + NORM_EPS)

    def centre_rows(t, carry):
        block = (gathered[pl.ds(8 * t, 8)].astype(F32) - centre[None]) * scale[None]
        wide_out[pl.ds(pl.multiple_of(t * 128, 128), 128), :] = block.reshape(128, 128)
        return carry

    lax.fori_loop(0, 16, centre_rows, 0, unroll=2)

    def project(jj, carry):
        x = wide_out[pl.ds(jj, 128, stride=16), :] * gain_col[...] + shift_col[...]
        out = jnp.dot(x.T.astype(BF16), w_out[...], preferred_element_type=F32)
        for j2 in range(2):
            for s, b in enumerate(BLOCK_ORDER):
                rows = pl.ds(b * 512 + j2 * 16 + jj, 16, stride=32)
                gate[rows, :] = gate[rows, :] * out[64 * j2 + 16 * s : 64 * j2 + 16 * s + 16]
        return carry

    lax.fori_loop(0, 16, project, 0, unroll=4)
    update[...] = gate[...].astype(BF16)


def on_device(pair, pair_mask, norm_gain, norm_shift, w_in, out_gain, out_shift, w_out, w_gate):
    vmem = pl.BlockSpec(memory_space=pltpu.VMEM)
    dma = pltpu.SemaphoreType.DMA
    out = pl.pallas_call(
        body,
        out_shape=jax.ShapeDtypeStruct((2048, 128), BF16),
        in_specs=[pl.BlockSpec(memory_space=pl.ANY)] * 9,
        out_specs=vmem,
        scratch_shapes=[
            pltpu.VMEM((2048, 128), BF16),
            pltpu.VMEM((32, 64), jnp.int32),
            pltpu.VMEM((1, 128), F32),
            pltpu.VMEM((1, 128), F32),
            pltpu.VMEM((128, 512), BF16),
            pltpu.VMEM((1, 128), F32),
            pltpu.VMEM((1, 128), F32),
            pltpu.VMEM((128, 128), BF16),
            pltpu.VMEM((128, 128), BF16),
            dma((9,)),
            pltpu.VMEM((2048, 128), F32),
            pltpu.VMEM((2048, 128), F32),
            pltpu.VMEM((2048, 128), F32),
            pltpu.VMEM((512, 128), BF16),
            pltpu.VMEM((16, 128), F32),
            pltpu.VMEM((16, 2, 4, 2, 16, 128), BF16),
            pltpu.VMEM((2, 2, 16, 16, 128), BF16),
            pltpu.VMEM((4, 2, 512, 128), BF16),
            pltpu.VMEM((4, 128, 512), BF16),
            pltpu.VMEM((8, 512, 128), BF16),
            pltpu.VMEM((8, 128, 512), BF16),
            pltpu.VMEM((8, 8, 2, 16, 128), BF16),
            pltpu.VMEM((128, 16, 128), BF16),
            pltpu.VMEM((2048, 128), F32),
            pltpu.VMEM((2048, 128), F32),
            pltpu.VMEM((128, 128), F32),
            pltpu.VMEM((128, 128), F32),
            dma, dma((4,)), dma((16,)), dma, dma((4,)),
            dma, dma, dma, dma, dma((4,)),
        ],
        compiler_params=pltpu.CompilerParams(
            collective_id=0, has_side_effects=True, vmem_limit_bytes=56 << 20
        ),
    )(
        pair.reshape(2048, 128), pair_mask.T, norm_gain.reshape(1, 128), norm_shift.reshape(1, 128), w_in,
        out_gain.reshape(1, 128), out_shift.reshape(1, 128), w_out, w_gate,
    )
    return out.reshape(64, 32, 128)


def solution(mesh):
    in_specs = (P("row", "col", None), P("row", "col"), P(), P(), P(), P(), P(), P(), P())
    out_specs = P("row", "col", None)
    return jax.shard_map(on_device, mesh=mesh, in_specs=in_specs, out_specs=out_specs, check_vma=False)
```

```python
import jax
import jax.numpy as jnp
from jax import lax
from jax.experimental import pallas as pl
from jax.experimental.pallas import tpu as pltpu
from jax.sharding import PartitionSpec as P

NORM_EPS = 1e-05
MESH = pl.DeviceIdType.MESH
ROWS, COLS = 16, 32
REACH = 4
F32, BF16 = jnp.float32, jnp.bfloat16
BLOCK_ORDER = (0, 2, 1, 3)


def slots(z, shift, lean):
    left = lax.rem(z - shift + 34 - lean, ROWS)
    right = lax.rem(z - shift + 22 - lean, ROWS)
    return lax.rem(left, 8), lax.rem(right, 8)


HAND_UP = ((1, 2), (1,))
HAND_DOWN = ((3,), (2, 3))


def body(
    pair_hbm, mask_hbm, norm_gain_hbm, norm_shift_hbm, w_in_hbm, out_gain_hbm, out_shift_hbm, w_out_hbm, w_gate_hbm,
    update,
    pair, mask, norm_gain, norm_shift, w_in, out_gain, out_shift, w_out, w_gate, load,
    normed, wide_left, wide_right, w_turned, mask_rows, own, left_row,
    col, right_turned, left_in, right_in, tiles, gathered, wide_out, gate,
    gain_col, shift_col,
    send_c, recv_c, send_l, recv_l, send_h, send_r, recv_r, send_g, send_t, recv_o, send_e, recv_e,
):
    z, d = lax.axis_index("row"), lax.axis_index("col")
    core = lax.rem(d, 2)

    operands = (
        (pair_hbm, pair), (mask_hbm, mask), (norm_gain_hbm, norm_gain), (norm_shift_hbm, norm_shift), (w_in_hbm, w_in),
        (out_gain_hbm, out_gain), (out_shift_hbm, out_shift), (w_out_hbm, w_out), (w_gate_hbm, w_gate),
    )
    loads = [pltpu.make_async_copy(src, dst, load.at[n]) for n, (src, dst) in enumerate(operands)]
    for copy in loads:
        copy.start()

    barrier = pltpu.get_barrier_semaphore()

    def greet_row(s, carry):
        pl.semaphore_signal(barrier, inc=1, device_id=(lax.rem(z + s, ROWS), d), device_id_type=MESH)
        return carry

    def greet_col(s, carry):
        pl.semaphore_signal(barrier, inc=1, device_id=(z, lax.rem(d + s, COLS)), device_id_type=MESH)
        return carry

    lax.fori_loop(1, REACH + 1, greet_row, 0)
    lax.fori_loop(ROWS - REACH, ROWS, greet_row, 0)
    lax.fori_loop(1, COLS, greet_col, 0)

    for copy in loads:
        copy.wait()

    def norm_rows(t, carry):
        rows = pl.ds(pl.multiple_of(t * 256, 256), 256)
        x = pair[rows, :].astype(F32)
        centred = x - jnp.mean(x, axis=-1, keepdims=True)
        second = jnp.mean(centred * centred, axis=-1, keepdims=True)
        normed[rows, :] = centred * lax.rsqrt(second + NORM_EPS) * norm_gain[...] + norm_shift[...]
        return carry

    lax.fori_loop(0, 8, norm_rows, 0)
    w_turned[...] = w_in[...].astype(F32).T.astype(BF16)
    valid = mask[...].astype(F32)
    valid = jnp.concatenate([valid.T[16 * b : 16 * b + 16] for b in BLOCK_ORDER], axis=0).T
    mask_rows[...] = jnp.concatenate([valid[0:16], valid[16:32]], axis=1)

    def panel_step(kk, carry):
        pieces = [
            normed[pl.ds(b * 512 + k2 * 16 + kk, 16, stride=32), :] for k2 in range(2) for b in BLOCK_ORDER
        ]
        x = jnp.concatenate(pieces, axis=0).astype(BF16)
        linear = lax.dot_general(w_turned[...], x, (((1,), (1,)), ((), ())), preferred_element_type=F32)
        m = mask_rows[pl.ds(kk, 1), :]
        wide_left[pl.ds(kk, 128, stride=16), :] = m * jax.nn.sigmoid(linear[128:256]) * linear[0:128]
        wide_right[pl.ds(kk, 128, stride=16), :] = m * jax.nn.sigmoid(linear[384:512]) * linear[256:384]
        return carry

    lax.fori_loop(0, 16, panel_step, 0)
    own[:, :, :, 0] = wide_left[...].astype(BF16).reshape(16, 2, 4, 16, 128)
    own[:, :, :, 1] = wide_right[...].astype(BF16).reshape(16, 2, 4, 16, 128)

    pl.semaphore_wait(barrier, 2 * REACH + COLS - 1)

    def route(c, i, side, end):
        shift = lax.rem(z + i, 4) + 4 * c
        slot = slots(z, shift, c)[side]
        to = lax.rem(z - slot + 2 - c + 4 * end + ROWS, ROWS)
        direct = (slot <= 6 - c) if end == 0 else (slot >= 2 - c)
        outer = (slot < 2 - c) | (slot > 6 - c)
        return to, 2 * i + slot // 4, direct, outer

    def launch(wanted, to, src, dst, send, recv):
        @pl.when(wanted & (to != z))
        def _():
            pltpu.make_async_remote_copy(
                src_ref=src, dst_ref=dst, send_sem=send, recv_sem=recv, device_id=(to, d), device_id_type=MESH
            ).start()

        @pl.when(wanted & (to == z))
        def _():
            pltpu.make_async_copy(src, dst, recv).start()

    def landed(wanted, to, src, dst, send, recv):
        @pl.when(wanted & (to != z))
        def _():
            pltpu.make_async_remote_copy(
                src_ref=src, dst_ref=dst, send_sem=send, recv_sem=recv, device_id=(to, d), device_id_type=MESH
            ).wait_send()

    my_q = lax.rem(z, 4)

    def corner_of(c):
        return lax.rem(z - my_q - 4 * c + ROWS, ROWS) // 4

    def hands_on(c, i, side):
        low = lax.rem(corner_of(c) + side, 2) == 0
        if i in HAND_UP[c] and i in HAND_DOWN[c]:
            return True, low
        if i in HAND_UP[c]:
            return low, low
        if i in HAND_DOWN[c]:
            return jnp.logical_not(low), low
        return None, low

    def hand_copy(low, buffer, at, send, recv):
        to = lax.rem(z + jnp.where(low, 4, 12), ROWS)
        place = buffer.at[at]
        return pltpu.make_async_remote_copy(
            src_ref=place, dst_ref=place, send_sem=send, recv_sem=recv, device_id=(to, d), device_id_type=MESH
        )

    def left_copy(c, i, end):
        to, at, direct, _ = route(c, i, 0, end)
        return (
            direct, to, own.at[:, c, lax.rem(z + i, 4), 0], left_row.at[at, c],
            send_l.at[8 * c + 2 * i + end], recv_l.at[2 * i + c],
        )

    def left_arrived(c, i):
        both = left_row.at[pl.ds(0, 2), 0]
        pltpu.make_async_copy(both, both, recv_l.at[2 * i + c]).wait()

    def left_hand(c, i):
        _, low = hands_on(c, i, 0)
        return hand_copy(low, left_row, (2 * i + jnp.where(low, 0, 1), c), send_h.at[2 * i + c], recv_l.at[2 * i + c])

    def left_out(i):
        for c in range(2):
            hands, _ = hands_on(c, i, 0)
            if hands is None:
                left_arrived(c, i)
            else:

                @pl.when(jnp.logical_not(hands))
                def _(c=c):
                    left_arrived(c, i)

        there = left_in.at[pl.ds(2 * i, 2), pl.ds(d * 16, 16), :]

        def one(s, carry):
            to = lax.rem(d + s, COLS)
            pltpu.make_async_remote_copy(
                src_ref=left_row.at[pl.ds(2 * i, 2), to % 2, to // 2], dst_ref=there,
                send_sem=send_e, recv_sem=recv_e, device_id=(z, to), device_id_type=MESH,
            ).start()
            return carry

        lax.fori_loop(1, COLS, one, 0)
        pltpu.make_async_copy(left_row.at[pl.ds(2 * i, 2), core, d // 2], there, recv_e).start()

    def spread_right():
        there = col.at[:, pl.ds(d * 16, 16), :]

        def one(s, carry):
            to = lax.rem(d + s, COLS)
            pltpu.make_async_remote_copy(
                src_ref=own.at[to // 2, to % 2, :, 1], dst_ref=there,
                send_sem=send_c, recv_sem=recv_c, device_id=(z, to), device_id_type=MESH,
            ).start()
            return carry

        lax.fori_loop(1, COLS, one, 0)
        pltpu.make_async_copy(own.at[d // 2, core, :, 1], there, recv_c).start()

    def on_core(work):
        for c in range(2):

            @pl.when(core == c)
            def _(c=c):
                work(c)

    def right_copy(c, i, end):
        to, at, direct, outer = route(c, i, 1, end)
        return outer, (
            direct, to, right_turned.at[lax.rem(z + i, 4)], right_in.at[at], send_r.at[2 * i + end], recv_r.at[i]
        )

    def right_arrived(i):
        both = right_in.at[pl.ds(0, 2)]
        pltpu.make_async_copy(both, both, recv_r.at[i]).wait()

    def right_hand(c, i):
        _, low = hands_on(c, i, 1)
        return hand_copy(low, right_in, 2 * i + jnp.where(low, 0, 1), send_g.at[i], recv_r.at[i])

    for i in (1, 3, 2, 0):
        for end in range(2):
            for c in range(2):
                launch(*left_copy(c, i, end))
    spread_right()

    for i in (1, 3, 2):
        for c in range(2):
            hands, _ = hands_on(c, i, 0)
            if hands is not None:

                @pl.when(hands)
                def _(c=c, i=i):
                    left_arrived(c, i)
                    left_hand(c, i).start()

    pltpu.make_async_copy(col, col, recv_c).wait()
    for q in range(4):
        right_turned[q] = col[q].astype(F32).T.astype(BF16)

    def first_rights(c):
        for i in (1, 3, 2):
            for end in range(2):
                outer, (direct, *rest) = right_copy(c, i, end)
                launch(direct & outer, *rest)

    def other_rights(c):
        for i in (1, 3, 2, 0):
            for end in range(2):
                outer, (direct, *rest) = right_copy(c, i, end)
                launch(direct & jnp.logical_not(outer), *rest)

    def hand_rights(c):
        for i in (1, 3, 2):
            hands, _ = hands_on(c, i, 1)
            if hands is not None:

                @pl.when(hands)
                def _(i=i):
                    right_arrived(i)
                    right_hand(c, i).start()

    on_core(first_rights)
    on_core(other_rights)
    left_out(0)

    def gate_rows(t, carry):
        rows = pl.ds(pl.multiple_of(t * 256, 256), 256)
        gate[rows, :] = jax.nn.sigmoid(
            jnp.dot(normed[rows, :].astype(BF16), w_gate[...], preferred_element_type=F32)
        )
        return carry

    lax.fori_loop(0, 8, gate_rows, 0)
    gain_col[...] = jnp.broadcast_to(out_gain[...], (128, 128)).T
    shift_col[...] = jnp.broadcast_to(out_shift[...], (128, 128)).T

    for i in (1, 3, 2):
        left_out(i)
    on_core(hand_rights)

    my_shift = my_q + 4 * core
    corner = lax.rem(z - my_shift + ROWS, ROWS) // 4
    my_left = corner // 2
    my_right = jnp.where(my_left == 0, corner, 3 - corner)
    left_base = lax.rem(my_shift - 2 + core + 8 * my_left + ROWS, ROWS)
    right_base = lax.rem(my_shift + 10 + core + 8 * my_right, ROWS)

    lanes_low = lax.broadcasted_iota(jnp.int32, (32, 128), 1) < 64

    def tile_send(i, h, a, half):
        row = lax.rem(left_base + lax.rem(10 - core - a // 2, 4) + 4 * (a % 2), ROWS)
        block = lax.rem(right_base + lax.rem(10 - core - i, 4) + 4 * h, ROWS)
        to = 2 * block + half
        src, dst = tiles.at[2 * i + h, a, half], gathered.at[4 * d + my_q]
        here = (row == z) & (to == d)

        @pl.when(jnp.logical_not(here))
        def _():
            pltpu.make_async_remote_copy(
                src_ref=src, dst_ref=dst, send_sem=send_t, recv_sem=recv_o, device_id=(row, to), device_id_type=MESH
            ).start()

        @pl.when(here)
        def _():
            pltpu.make_async_copy(src, dst, recv_o).start()

    def multiply(i, h):
        right = right_in[2 * i + h]
        for pair_index in range(4):
            both = jnp.concatenate([left_in[2 * pair_index], left_in[2 * pair_index + 1]], axis=1)
            grid = jnp.dot(right, both, preferred_element_type=F32)
            for side in range(2):
                m = grid[:, 128 * side : 128 * side + 128]
                kept = jnp.where(lanes_low, m[0:32], m[96:128])
                moved = jnp.where(lanes_low, m[32:64], m[64:96])
                tile = (kept + pltpu.roll(moved, 64, axis=1)).astype(BF16)
                a = 2 * pair_index + side
                tiles[2 * i + h, a] = tile.reshape(2, 16, 128)
                for half in range(2):
                    tile_send(i, h, a, half)

    pltpu.make_async_copy(left_in, left_in, recv_e).wait()

    for i in (1, 3, 2, 0):
        waiting = jnp.array(True)
        for c in range(2):
            hands, _ = hands_on(c, i, 1)
            if hands is not None:
                waiting = waiting & jnp.logical_not((core == c) & hands)

        @pl.when(waiting)
        def _(i=i):
            right_arrived(i)

        def half_rank(h, carry, i=i):
            multiply(i, h)
            return carry

        lax.fori_loop(0, 2, half_rank, 0)

    def gone(buffer, sem):
        pltpu.make_async_copy(buffer, buffer, sem).wait()

    gone(col.at[:, pl.ds(0, 31 * 16)], send_c)
    gone(left_in.at[:, pl.ds(0, 31 * 16)], send_e)
    for i in range(4):
        for c in range(2):
            for end in range(2):
                landed(*left_copy(c, i, end))
            hands, _ = hands_on(c, i, 0)
            if hands is not None:

                @pl.when(hands)
                def _(c=c, i=i):
                    left_hand(c, i).wait_send()

    def rights_gone(c):
        for i in range(4):
            for end in range(2):
                landed(*right_copy(c, i, end)[1])
            hands, _ = hands_on(c, i, 1)
            if hands is not None:

                @pl.when(hands)
                def _(i=i):
                    right_hand(c, i).wait_send()

    on_core(rights_gone)
    gone(gathered.at[pl.ds(0, 127)], send_t)

    @pl.when(lax.rem(d // 2 - right_base + 2 * ROWS, ROWS) >= 8)
    def _():
        gone(gathered.at[0], send_t)

    pltpu.make_async_copy(gathered, gathered, recv_o).wait()

    def total(t, carry):
        block = gathered[pl.ds(8 * t, 8)].astype(F32)
        return carry + jnp.sum(block, axis=0)

    centre = lax.fori_loop(0, 16, total, jnp.zeros((16, 128), F32)) * (1.0 / 128)

    def squares(t, carry):
        block = gathered[pl.ds(8 * t, 8)].astype(F32) - centre[None]
        return carry + jnp.sum(block * block, axis=0)

    second = lax.fori_loop(0, 16, squares, jnp.zeros((16, 128), F32)) * (1.0 / 128)
    scale = lax.rsqrt(second + NORM_EPS)

    def centre_rows(t, carry):
        block = (gathered[pl.ds(8 * t, 8)].astype(F32) - centre[None]) * scale[None]
        wide_out[pl.ds(pl.multiple_of(t * 128, 128), 128), :] = block.reshape(128, 128)
        return carry

    lax.fori_loop(0, 16, centre_rows, 0, unroll=2)

    def project(jj, carry):
        x = wide_out[pl.ds(jj, 128, stride=16), :] * gain_col[...] + shift_col[...]
        out = jnp.dot(x.T.astype(BF16), w_out[...], preferred_element_type=F32)
        for j2 in range(2):
            for s, b in enumerate(BLOCK_ORDER):
                rows = pl.ds(b * 512 + j2 * 16 + jj, 16, stride=32)
                gate[rows, :] = gate[rows, :] * out[64 * j2 + 16 * s : 64 * j2 + 16 * s + 16]
        return carry

    lax.fori_loop(0, 16, project, 0, unroll=4)
    update[...] = gate[...].astype(BF16)


def on_device(pair, pair_mask, norm_gain, norm_shift, w_in, out_gain, out_shift, w_out, w_gate):
    vmem = pl.BlockSpec(memory_space=pltpu.VMEM)
    dma = pltpu.SemaphoreType.DMA
    out = pl.pallas_call(
        body,
        out_shape=jax.ShapeDtypeStruct((2048, 128), BF16),
        in_specs=[pl.BlockSpec(memory_space=pl.ANY)] * 9,
        out_specs=vmem,
        scratch_shapes=[
            pltpu.VMEM((2048, 128), BF16),
            pltpu.VMEM((32, 64), jnp.int32),
            pltpu.VMEM((1, 128), F32),
            pltpu.VMEM((1, 128), F32),
            pltpu.VMEM((128, 512), BF16),
            pltpu.VMEM((1, 128), F32),
            pltpu.VMEM((1, 128), F32),
            pltpu.VMEM((128, 128), BF16),
            pltpu.VMEM((128, 128), BF16),
            dma((9,)),
            pltpu.VMEM((2048, 128), F32),
            pltpu.VMEM((2048, 128), F32),
            pltpu.VMEM((2048, 128), F32),
            pltpu.VMEM((512, 128), BF16),
            pltpu.VMEM((16, 128), F32),
            pltpu.VMEM((16, 2, 4, 2, 16, 128), BF16),
            pltpu.VMEM((8, 2, 16, 16, 128), BF16),
            pltpu.VMEM((4, 512, 128), BF16),
            pltpu.VMEM((4, 128, 512), BF16),
            pltpu.VMEM((8, 512, 128), BF16),
            pltpu.VMEM((8, 128, 512), BF16),
            pltpu.VMEM((8, 8, 2, 16, 128), BF16),
            pltpu.VMEM((128, 16, 128), BF16),
            pltpu.VMEM((2048, 128), F32),
            pltpu.VMEM((2048, 128), F32),
            pltpu.VMEM((128, 128), F32),
            pltpu.VMEM((128, 128), F32),
            dma, dma, dma((16,)), dma((8,)), dma((8,)),
            dma((8,)), dma((4,)), dma((4,)),
            dma, dma, dma, dma,
        ],
        compiler_params=pltpu.CompilerParams(
            collective_id=0, has_side_effects=True, vmem_limit_bytes=56 << 20
        ),
    )(
        pair.reshape(2048, 128), pair_mask.T, norm_gain.reshape(1, 128), norm_shift.reshape(1, 128), w_in,
        out_gain.reshape(1, 128), out_shift.reshape(1, 128), w_out, w_gate,
    )
    return out.reshape(64, 32, 128)


def solution(mesh):
    in_specs = (P("row", "col", None), P("row", "col"), P(), P(), P(), P(), P(), P(), P())
    out_specs = P("row", "col", None)
    return jax.shard_map(on_device, mesh=mesh, in_specs=in_specs, out_specs=out_specs, check_vma=False)
```

```python
import jax
import jax.numpy as jnp
from jax import lax
from jax.experimental import pallas as pl
from jax.experimental.pallas import tpu as pltpu
from jax.sharding import PartitionSpec as P

NORM_EPS = 1e-05
MESH = pl.DeviceIdType.MESH
ROWS, COLS = 16, 32
REACH = 4
F32, BF16 = jnp.float32, jnp.bfloat16
BLOCK_ORDER = (0, 2, 1, 3)


def slots(z, shift, lean):
    left = lax.rem(z - shift + 34 - lean, ROWS)
    right = lax.rem(z - shift + 22 - lean, ROWS)
    return lax.rem(left, 8), lax.rem(right, 8)


HAND_UP = ((1, 2), (1,))
HAND_DOWN = ((3,), (2, 3))


def body(
    pair_hbm, mask_hbm, norm_gain_hbm, norm_shift_hbm, w_in_hbm, out_gain_hbm, out_shift_hbm, w_out_hbm, w_gate_hbm,
    update,
    pair, mask, norm_gain, norm_shift, w_in, out_gain, out_shift, w_out, w_gate, load,
    normed, wide_left, wide_right, w_turned, mask_rows, own, left_row,
    col, right_turned, left_in, right_in, tiles, gathered, wide_out, gate,
    gain_col, shift_col,
    send_c, recv_c, send_l, recv_l, send_h, send_r, recv_r, send_g, send_t, recv_o, send_e, recv_e,
):
    z, d = lax.axis_index("row"), lax.axis_index("col")
    core = lax.rem(d, 2)

    operands = (
        (pair_hbm, pair), (mask_hbm, mask), (norm_gain_hbm, norm_gain), (norm_shift_hbm, norm_shift), (w_in_hbm, w_in),
        (out_gain_hbm, out_gain), (out_shift_hbm, out_shift), (w_out_hbm, w_out), (w_gate_hbm, w_gate),
    )
    loads = [pltpu.make_async_copy(src, dst, load.at[n]) for n, (src, dst) in enumerate(operands)]
    for copy in loads:
        copy.start()

    barrier = pltpu.get_barrier_semaphore()

    def greet_row(s, carry):
        pl.semaphore_signal(barrier, inc=1, device_id=(lax.rem(z + s, ROWS), d), device_id_type=MESH)
        return carry

    def greet_col(s, carry):
        pl.semaphore_signal(barrier, inc=1, device_id=(z, lax.rem(d + s, COLS)), device_id_type=MESH)
        return carry

    lax.fori_loop(1, REACH + 1, greet_row, 0)
    lax.fori_loop(ROWS - REACH, ROWS, greet_row, 0)
    lax.fori_loop(1, COLS, greet_col, 0)

    for copy in loads:
        copy.wait()

    def norm_rows(t, carry):
        rows = pl.ds(pl.multiple_of(t * 256, 256), 256)
        x = pair[rows, :].astype(F32)
        centred = x - jnp.mean(x, axis=-1, keepdims=True)
        second = jnp.mean(centred * centred, axis=-1, keepdims=True)
        normed[rows, :] = centred * lax.rsqrt(second + NORM_EPS) * norm_gain[...] + norm_shift[...]
        return carry

    lax.fori_loop(0, 8, norm_rows, 0)
    w_turned[...] = w_in[...].astype(F32).T.astype(BF16)
    valid = mask[...].astype(F32)
    valid = jnp.concatenate([valid.T[16 * b : 16 * b + 16] for b in BLOCK_ORDER], axis=0).T
    mask_rows[...] = jnp.concatenate([valid[0:16], valid[16:32]], axis=1)

    def panel_step(kk, carry):
        pieces = [
            normed[pl.ds(b * 512 + k2 * 16 + kk, 16, stride=32), :] for k2 in range(2) for b in BLOCK_ORDER
        ]
        x = jnp.concatenate(pieces, axis=0).astype(BF16)
        linear = lax.dot_general(w_turned[...], x, (((1,), (1,)), ((), ())), preferred_element_type=F32)
        m = mask_rows[pl.ds(kk, 1), :]
        wide_left[pl.ds(kk, 128, stride=16), :] = m * jax.nn.sigmoid(linear[128:256]) * linear[0:128]
        wide_right[pl.ds(kk, 128, stride=16), :] = m * jax.nn.sigmoid(linear[384:512]) * linear[256:384]
        return carry

    lax.fori_loop(0, 16, panel_step, 0)
    for side, wide in enumerate((wide_left, wide_right)):
        panel = wide[...].astype(BF16).reshape(16, 2, 4, 16, 128)
        for c in range(2):
            for q in range(4):
                own[c, q, side] = panel[:, c, q]

    pl.semaphore_wait(barrier, 2 * REACH + COLS - 1)

    def route(c, i, side, end):
        shift = lax.rem(z + i, 4) + 4 * c
        slot = slots(z, shift, c)[side]
        to = lax.rem(z - slot + 2 - c + 4 * end + ROWS, ROWS)
        direct = (slot <= 6 - c) if end == 0 else (slot >= 2 - c)
        outer = (slot < 2 - c) | (slot > 6 - c)
        return to, 2 * i + slot // 4, direct, outer

    def launch(wanted, to, src, dst, send, recv):
        @pl.when(wanted & (to != z))
        def _():
            pltpu.make_async_remote_copy(
                src_ref=src, dst_ref=dst, send_sem=send, recv_sem=recv, device_id=(to, d), device_id_type=MESH
            ).start()

        @pl.when(wanted & (to == z))
        def _():
            pltpu.make_async_copy(src, dst, recv).start()

    def landed(wanted, to, src, dst, send, recv):
        @pl.when(wanted & (to != z))
        def _():
            pltpu.make_async_remote_copy(
                src_ref=src, dst_ref=dst, send_sem=send, recv_sem=recv, device_id=(to, d), device_id_type=MESH
            ).wait_send()

    my_q = lax.rem(z, 4)

    def corner_of(c):
        return lax.rem(z - my_q - 4 * c + ROWS, ROWS) // 4

    def hands_on(c, i, side):
        low = lax.rem(corner_of(c) + side, 2) == 0
        if i in HAND_UP[c] and i in HAND_DOWN[c]:
            return True, low
        if i in HAND_UP[c]:
            return low, low
        if i in HAND_DOWN[c]:
            return jnp.logical_not(low), low
        return None, low

    def hand_copy(low, buffer, at, send, recv):
        to = lax.rem(z + jnp.where(low, 4, 12), ROWS)
        place = buffer.at[at]
        return pltpu.make_async_remote_copy(
            src_ref=place, dst_ref=place, send_sem=send, recv_sem=recv, device_id=(to, d), device_id_type=MESH
        )

    def left_copy(c, i, end):
        to, at, direct, _ = route(c, i, 0, end)
        return (
            direct, to, own.at[c, lax.rem(z + i, 4), 0], left_row.at[at, c],
            send_l.at[8 * c + 2 * i + end], recv_l.at[2 * at + c],
        )

    def left_arrived(c, at):
        block = left_row.at[at, c]
        pltpu.make_async_copy(block, block, recv_l.at[2 * at + c]).wait()

    def left_hand(c, i):
        _, low = hands_on(c, i, 0)
        at = 2 * i + jnp.where(low, 0, 1)
        return at, hand_copy(low, left_row, (at, c), send_h.at[2 * i + c], recv_l.at[2 * at + c])

    def left_out(i):
        for c in range(2):
            hands, low = hands_on(c, i, 0)
            for h in range(2):
                if hands is None:
                    left_arrived(c, 2 * i + h)
                else:
                    handed = hands & (jnp.logical_not(low) if h else low)

                    @pl.when(jnp.logical_not(handed))
                    def _(c=c, h=h):
                        left_arrived(c, 2 * i + h)

        there = left_in.at[pl.ds(2 * i, 2), pl.ds(d * 16, 16), :]

        def one(s, carry):
            to = lax.rem(d + s, COLS)
            pltpu.make_async_remote_copy(
                src_ref=left_row.at[pl.ds(2 * i, 2), to % 2, to // 2], dst_ref=there,
                send_sem=send_e, recv_sem=recv_e, device_id=(z, to), device_id_type=MESH,
            ).start()
            return carry

        lax.fori_loop(1, COLS, one, 0)
        pltpu.make_async_copy(left_row.at[pl.ds(2 * i, 2), core, d // 2], there, recv_e).start()

    def spread_right():
        there = col.at[:, pl.ds(d * 16, 16), :]

        def one(s, carry):
            to = lax.rem(d + s, COLS)
            pltpu.make_async_remote_copy(
                src_ref=own.at[to % 2, :, 1, to // 2], dst_ref=there,
                send_sem=send_c, recv_sem=recv_c, device_id=(z, to), device_id_type=MESH,
            ).start()
            return carry

        lax.fori_loop(1, COLS, one, 0)
        pltpu.make_async_copy(own.at[core, :, 1, d // 2], there, recv_c).start()

    def on_core(work):
        for c in range(2):

            @pl.when(core == c)
            def _(c=c):
                work(c)

    def right_copy(c, i, end):
        to, at, direct, outer = route(c, i, 1, end)
        return outer, (
            direct, to, right_turned.at[lax.rem(z + i, 4)], right_in.at[at], send_r.at[2 * i + end], recv_r.at[at]
        )

    def right_arrived(at):
        pltpu.make_async_copy(right_in.at[at], right_in.at[at], recv_r.at[at]).wait()

    def right_hand(c, i):
        _, low = hands_on(c, i, 1)
        at = 2 * i + jnp.where(low, 0, 1)
        return at, hand_copy(low, right_in, at, send_g.at[i], recv_r.at[at])

    for first in (True, False):
        for i in (1, 3, 2, 0)[: 3 if first else 4]:
            for end in range(2):
                for c in range(2):
                    outer = route(c, i, 0, end)[3]
                    direct, *rest = left_copy(c, i, end)
                    launch(direct & (outer if first else jnp.logical_not(outer)), *rest)
    spread_right()

    for i in (1, 3, 2):
        for c in range(2):
            hands, _ = hands_on(c, i, 0)
            if hands is not None:

                @pl.when(hands)
                def _(c=c, i=i):
                    at, copy = left_hand(c, i)
                    left_arrived(c, at)
                    copy.start()

    pltpu.make_async_copy(col, col, recv_c).wait()
    for q in range(4):
        right_turned[q] = col[q].astype(F32).T.astype(BF16)

    def first_rights(c):
        for i in (1, 3, 2):
            for end in range(2):
                outer, (direct, *rest) = right_copy(c, i, end)
                launch(direct & outer, *rest)

    def other_rights(c, ranks):
        for i in ranks:
            for end in range(2):
                outer, (direct, *rest) = right_copy(c, i, end)
                launch(direct & jnp.logical_not(outer), *rest)

    def hand_rights(c):
        for i in (1, 3, 2):
            hands, _ = hands_on(c, i, 1)
            if hands is not None:

                @pl.when(hands)
                def _(i=i):
                    at, copy = right_hand(c, i)
                    right_arrived(at)
                    copy.start()

    on_core(first_rights)
    on_core(lambda c: other_rights(c, (1, 3)))
    left_out(0)

    def gate_rows(t, carry):
        rows = pl.ds(pl.multiple_of(t * 256, 256), 256)
        gate[rows, :] = jax.nn.sigmoid(
            jnp.dot(normed[rows, :].astype(BF16), w_gate[...], preferred_element_type=F32)
        )
        return carry

    lax.fori_loop(0, 8, gate_rows, 0)
    gain_col[...] = jnp.broadcast_to(out_gain[...], (128, 128)).T
    shift_col[...] = jnp.broadcast_to(out_shift[...], (128, 128)).T

    on_core(hand_rights)
    on_core(lambda c: other_rights(c, (2,)))
    left_out(1)
    left_out(3)
    on_core(lambda c: other_rights(c, (0,)))
    left_out(2)

    my_shift = my_q + 4 * core
    corner = lax.rem(z - my_shift + ROWS, ROWS) // 4
    my_left = corner // 2
    my_right = jnp.where(my_left == 0, corner, 3 - corner)
    left_base = lax.rem(my_shift - 2 + core + 8 * my_left + ROWS, ROWS)
    right_base = lax.rem(my_shift + 10 + core + 8 * my_right, ROWS)

    lanes_low = lax.broadcasted_iota(jnp.int32, (32, 128), 1) < 64

    def tile_send(i, h, a, half):
        row = lax.rem(left_base + lax.rem(10 - core - a // 2, 4) + 4 * (a % 2), ROWS)
        block = lax.rem(right_base + lax.rem(10 - core - i, 4) + 4 * h, ROWS)
        to = 2 * block + half
        src, dst = tiles.at[2 * i + h, a, half], gathered.at[4 * d + my_q]
        here = (row == z) & (to == d)

        @pl.when(jnp.logical_not(here))
        def _():
            pltpu.make_async_remote_copy(
                src_ref=src, dst_ref=dst, send_sem=send_t, recv_sem=recv_o, device_id=(row, to), device_id_type=MESH
            ).start()

        @pl.when(here)
        def _():
            pltpu.make_async_copy(src, dst, recv_o).start()

    def multiply(i, h):
        right = right_in[2 * i + h]
        for pair_index in range(4):
            both = jnp.concatenate([left_in[2 * pair_index], left_in[2 * pair_index + 1]], axis=1)
            grid = jnp.dot(right, both, preferred_element_type=F32)
            for side in range(2):
                m = grid[:, 128 * side : 128 * side + 128]
                kept = jnp.where(lanes_low, m[0:32], m[96:128])
                moved = jnp.where(lanes_low, m[32:64], m[64:96])
                tile = (kept + pltpu.roll(moved, 64, axis=1)).astype(BF16)
                a = 2 * pair_index + side
                tiles[2 * i + h, a] = tile.reshape(2, 16, 128)
                for half in range(2):
                    tile_send(i, h, a, half)

    pltpu.make_async_copy(left_in, left_in, recv_e).wait()

    for i in (1, 3, 2, 0):
        for h in range(2):
            waiting = jnp.array(True)
            for c in range(2):
                hands, low = hands_on(c, i, 1)
                if hands is not None:
                    handed = hands & (jnp.logical_not(low) if h else low)
                    waiting = waiting & jnp.logical_not((core == c) & handed)

            @pl.when(waiting)
            def _(i=i, h=h):
                right_arrived(2 * i + h)

        def half_rank(h, carry, i=i):
            multiply(i, h)
            return carry

        lax.fori_loop(0, 2, half_rank, 0)

    def gone(buffer, sem):
        pltpu.make_async_copy(buffer, buffer, sem).wait()

    gone(col.at[:, pl.ds(0, 31 * 16)], send_c)
    gone(left_in.at[:, pl.ds(0, 31 * 16)], send_e)
    for i in range(4):
        for c in range(2):
            for end in range(2):
                landed(*left_copy(c, i, end))
            hands, _ = hands_on(c, i, 0)
            if hands is not None:

                @pl.when(hands)
                def _(c=c, i=i):
                    left_hand(c, i)[1].wait_send()

    def rights_gone(c):
        for i in range(4):
            for end in range(2):
                landed(*right_copy(c, i, end)[1])
            hands, _ = hands_on(c, i, 1)
            if hands is not None:

                @pl.when(hands)
                def _(i=i):
                    right_hand(c, i)[1].wait_send()

    on_core(rights_gone)
    gone(gathered.at[pl.ds(0, 127)], send_t)

    @pl.when(lax.rem(d // 2 - right_base + 2 * ROWS, ROWS) >= 8)
    def _():
        gone(gathered.at[0], send_t)

    pltpu.make_async_copy(gathered, gathered, recv_o).wait()

    def total(t, carry):
        block = gathered[pl.ds(8 * t, 8)].astype(F32)
        return carry + jnp.sum(block, axis=0)

    centre = lax.fori_loop(0, 16, total, jnp.zeros((16, 128), F32)) * (1.0 / 128)

    def squares(t, carry):
        block = gathered[pl.ds(8 * t, 8)].astype(F32) - centre[None]
        return carry + jnp.sum(block * block, axis=0)

    second = lax.fori_loop(0, 16, squares, jnp.zeros((16, 128), F32)) * (1.0 / 128)
    scale = lax.rsqrt(second + NORM_EPS)

    def centre_rows(t, carry):
        block = (gathered[pl.ds(8 * t, 8)].astype(F32) - centre[None]) * scale[None]
        wide_out[pl.ds(pl.multiple_of(t * 128, 128), 128), :] = block.reshape(128, 128)
        return carry

    lax.fori_loop(0, 16, centre_rows, 0, unroll=2)

    def project(jj, carry):
        x = wide_out[pl.ds(jj, 128, stride=16), :] * gain_col[...] + shift_col[...]
        out = jnp.dot(x.T.astype(BF16), w_out[...], preferred_element_type=F32)
        for j2 in range(2):
            for s, b in enumerate(BLOCK_ORDER):
                rows = pl.ds(b * 512 + j2 * 16 + jj, 16, stride=32)
                gate[rows, :] = gate[rows, :] * out[64 * j2 + 16 * s : 64 * j2 + 16 * s + 16]
        return carry

    lax.fori_loop(0, 16, project, 0, unroll=4)
    update[...] = gate[...].astype(BF16)


def on_device(pair, pair_mask, norm_gain, norm_shift, w_in, out_gain, out_shift, w_out, w_gate):
    vmem = pl.BlockSpec(memory_space=pltpu.VMEM)
    dma = pltpu.SemaphoreType.DMA
    out = pl.pallas_call(
        body,
        out_shape=jax.ShapeDtypeStruct((2048, 128), BF16),
        in_specs=[pl.BlockSpec(memory_space=pl.ANY)] * 9,
        out_specs=vmem,
        scratch_shapes=[
            pltpu.VMEM((2048, 128), BF16),
            pltpu.VMEM((32, 64), jnp.int32),
            pltpu.VMEM((1, 128), F32),
            pltpu.VMEM((1, 128), F32),
            pltpu.VMEM((128, 512), BF16),
            pltpu.VMEM((1, 128), F32),
            pltpu.VMEM((1, 128), F32),
            pltpu.VMEM((128, 128), BF16),
            pltpu.VMEM((128, 128), BF16),
            dma((9,)),
            pltpu.VMEM((2048, 128), F32),
            pltpu.VMEM((2048, 128), F32),
            pltpu.VMEM((2048, 128), F32),
            pltpu.VMEM((512, 128), BF16),
            pltpu.VMEM((16, 128), F32),
            pltpu.VMEM((2, 4, 2, 16, 16, 128), BF16),
            pltpu.VMEM((8, 2, 16, 16, 128), BF16),
            pltpu.VMEM((4, 512, 128), BF16),
            pltpu.VMEM((4, 128, 512), BF16),
            pltpu.VMEM((8, 512, 128), BF16),
            pltpu.VMEM((8, 128, 512), BF16),
            pltpu.VMEM((8, 8, 2, 16, 128), BF16),
            pltpu.VMEM((128, 16, 128), BF16),
            pltpu.VMEM((2048, 128), F32),
            pltpu.VMEM((2048, 128), F32),
            pltpu.VMEM((128, 128), F32),
            pltpu.VMEM((128, 128), F32),
            dma, dma, dma((16,)), dma((16,)), dma((8,)),
            dma((8,)), dma((8,)), dma((4,)),
            dma, dma, dma, dma,
        ],
        compiler_params=pltpu.CompilerParams(
            collective_id=0, has_side_effects=True, vmem_limit_bytes=56 << 20
        ),
    )(
        pair.reshape(2048, 128), pair_mask.T, norm_gain.reshape(1, 128), norm_shift.reshape(1, 128), w_in,
        out_gain.reshape(1, 128), out_shift.reshape(1, 128), w_out, w_gate,
    )
    return out.reshape(64, 32, 128)


def solution(mesh):
    in_specs = (P("row", "col", None), P("row", "col"), P(), P(), P(), P(), P(), P(), P())
    out_specs = P("row", "col", None)
    return jax.shard_map(on_device, mesh=mesh, in_specs=in_specs, out_specs=out_specs, check_vma=False)
```

```python
import jax
import jax.numpy as jnp
from jax import lax
from jax.experimental import pallas as pl
from jax.experimental.pallas import tpu as pltpu
from jax.sharding import PartitionSpec as P

NORM_EPS = 1e-05
MESH = pl.DeviceIdType.MESH
ROWS, COLS = 16, 32
REACH = 4
F32, BF16 = jnp.float32, jnp.bfloat16
BLOCK_ORDER = (0, 2, 1, 3)


def slots(z, shift, lean):
    left = lax.rem(z - shift + 34 - lean, ROWS)
    right = lax.rem(z - shift + 22 - lean, ROWS)
    return lax.rem(left, 8), lax.rem(right, 8)


HAND_UP = ((1, 2), (1,))
HAND_DOWN = ((3,), (2, 3))


def body(
    pair_hbm, mask_hbm, norm_gain_hbm, norm_shift_hbm, w_in_hbm, out_gain_hbm, out_shift_hbm, w_out_hbm, w_gate_hbm,
    update,
    pair, mask, norm_gain, norm_shift, w_in, out_gain, out_shift, w_out, w_gate, load,
    normed, wide_left, wide_right, w_turned, mask_rows, own, left_row,
    col, right_turned, left_in, right_in, tiles, gathered, wide_out, gate,
    gain_col, shift_col,
    send_c, recv_c, send_l, recv_l, send_h, send_r, recv_r, send_g, send_t, recv_o, send_e, recv_e,
):
    z, d = lax.axis_index("row"), lax.axis_index("col")
    core = lax.rem(d, 2)

    operands = (
        (pair_hbm, pair), (mask_hbm, mask), (norm_gain_hbm, norm_gain), (norm_shift_hbm, norm_shift), (w_in_hbm, w_in),
        (out_gain_hbm, out_gain), (out_shift_hbm, out_shift), (w_out_hbm, w_out), (w_gate_hbm, w_gate),
    )
    loads = [pltpu.make_async_copy(src, dst, load.at[n]) for n, (src, dst) in enumerate(operands)]
    for copy in loads:
        copy.start()

    barrier = pltpu.get_barrier_semaphore()

    def greet_row(s, carry):
        pl.semaphore_signal(barrier, inc=1, device_id=(lax.rem(z + s, ROWS), d), device_id_type=MESH)
        return carry

    def greet_col(s, carry):
        pl.semaphore_signal(barrier, inc=1, device_id=(z, lax.rem(d + s, COLS)), device_id_type=MESH)
        return carry

    lax.fori_loop(1, REACH + 1, greet_row, 0)
    lax.fori_loop(ROWS - REACH, ROWS, greet_row, 0)
    lax.fori_loop(1, COLS, greet_col, 0)

    for copy in loads:
        copy.wait()

    def norm_rows(t, carry):
        rows = pl.ds(pl.multiple_of(t * 256, 256), 256)
        x = pair[rows, :].astype(F32)
        centred = x - jnp.mean(x, axis=-1, keepdims=True)
        second = jnp.mean(centred * centred, axis=-1, keepdims=True)
        normed[rows, :] = centred * lax.rsqrt(second + NORM_EPS) * norm_gain[...] + norm_shift[...]
        return carry

    lax.fori_loop(0, 8, norm_rows, 0)
    w_turned[...] = w_in[...].astype(F32).T.astype(BF16)
    valid = mask[...].astype(F32)
    valid = jnp.concatenate([valid.T[16 * b : 16 * b + 16] for b in BLOCK_ORDER], axis=0).T
    mask_rows[...] = jnp.concatenate([valid[0:16], valid[16:32]], axis=1)

    def panel_step(kk, carry):
        pieces = [
            normed[pl.ds(b * 512 + k2 * 16 + kk, 16, stride=32), :] for k2 in range(2) for b in BLOCK_ORDER
        ]
        x = jnp.concatenate(pieces, axis=0).astype(BF16)
        linear = lax.dot_general(w_turned[...], x, (((1,), (1,)), ((), ())), preferred_element_type=F32)
        m = mask_rows[pl.ds(kk, 1), :]
        wide_left[pl.ds(kk, 128, stride=16), :] = m * jax.nn.sigmoid(linear[128:256]) * linear[0:128]
        wide_right[pl.ds(kk, 128, stride=16), :] = m * jax.nn.sigmoid(linear[384:512]) * linear[256:384]
        return carry

    lax.fori_loop(0, 16, panel_step, 0)
    for side, wide in enumerate((wide_left, wide_right)):
        panel = wide[...].astype(BF16).reshape(16, 2, 4, 16, 128)
        for c in range(2):
            for q in range(4):
                own[c, q, side] = panel[:, c, q]

    pl.semaphore_wait(barrier, 2 * REACH + COLS - 1)

    def route(c, i, side, end):
        shift = lax.rem(z + i, 4) + 4 * c
        slot = slots(z, shift, c)[side]
        to = lax.rem(z - slot + 2 - c + 4 * end + ROWS, ROWS)
        direct = (slot <= 6 - c) if end == 0 else (slot >= 2 - c)
        outer = (slot < 2 - c) | (slot > 6 - c)
        return to, 2 * i + slot // 4, direct, outer

    def launch(wanted, to, src, dst, send, recv):
        @pl.when(wanted & (to != z))
        def _():
            pltpu.make_async_remote_copy(
                src_ref=src, dst_ref=dst, send_sem=send, recv_sem=recv, device_id=(to, d), device_id_type=MESH
            ).start()

        @pl.when(wanted & (to == z))
        def _():
            pltpu.make_async_copy(src, dst, recv).start()

    def landed(wanted, to, src, dst, send, recv):
        @pl.when(wanted & (to != z))
        def _():
            pltpu.make_async_remote_copy(
                src_ref=src, dst_ref=dst, send_sem=send, recv_sem=recv, device_id=(to, d), device_id_type=MESH
            ).wait_send()

    my_q = lax.rem(z, 4)

    def corner_of(c):
        return lax.rem(z - my_q - 4 * c + ROWS, ROWS) // 4

    def hands_on(c, i, side):
        low = lax.rem(corner_of(c) + side, 2) == 0
        if i in HAND_UP[c] and i in HAND_DOWN[c]:
            return True, low
        if i in HAND_UP[c]:
            return low, low
        if i in HAND_DOWN[c]:
            return jnp.logical_not(low), low
        return None, low

    def hand_copy(low, buffer, at, send, recv):
        to = lax.rem(z + jnp.where(low, 4, 12), ROWS)
        place = buffer.at[at]
        return pltpu.make_async_remote_copy(
            src_ref=place, dst_ref=place, send_sem=send, recv_sem=recv, device_id=(to, d), device_id_type=MESH
        )

    def left_copy(c, i, end):
        to, at, direct, _ = route(c, i, 0, end)
        return (
            direct, to, own.at[c, lax.rem(z + i, 4), 0], left_row.at[at, c],
            send_l.at[8 * c + 2 * i + end], recv_l.at[2 * at + c],
        )

    def left_arrived(c, at):
        block = left_row.at[at, c]
        pltpu.make_async_copy(block, block, recv_l.at[2 * at + c]).wait()

    def left_hand(c, i):
        _, low = hands_on(c, i, 0)
        at = 2 * i + jnp.where(low, 0, 1)
        return at, hand_copy(low, left_row, (at, c), send_h.at[2 * i + c], recv_l.at[2 * at + c])

    def left_out(i):
        for c in range(2):
            hands, low = hands_on(c, i, 0)
            for h in range(2):
                if hands is None:
                    left_arrived(c, 2 * i + h)
                else:
                    handed = hands & (jnp.logical_not(low) if h else low)

                    @pl.when(jnp.logical_not(handed))
                    def _(c=c, h=h):
                        left_arrived(c, 2 * i + h)

        there = left_in.at[pl.ds(2 * i, 2), pl.ds(d * 16, 16), :]

        def one(s, carry):
            to = lax.rem(d + s, COLS)
            pltpu.make_async_remote_copy(
                src_ref=left_row.at[pl.ds(2 * i, 2), to % 2, to // 2], dst_ref=there,
                send_sem=send_e, recv_sem=recv_e, device_id=(z, to), device_id_type=MESH,
            ).start()
            return carry

        lax.fori_loop(1, COLS, one, 0)
        pltpu.make_async_copy(left_row.at[pl.ds(2 * i, 2), core, d // 2], there, recv_e).start()

    def spread_right():
        there = col.at[:, pl.ds(d * 16, 16), :]

        def one(s, carry):
            to = lax.rem(d + s, COLS)
            pltpu.make_async_remote_copy(
                src_ref=own.at[to % 2, :, 1, to // 2], dst_ref=there,
                send_sem=send_c, recv_sem=recv_c, device_id=(z, to), device_id_type=MESH,
            ).start()
            return carry

        lax.fori_loop(1, COLS, one, 0)
        pltpu.make_async_copy(own.at[core, :, 1, d // 2], there, recv_c).start()

    def on_core(work):
        for c in range(2):

            @pl.when(core == c)
            def _(c=c):
                work(c)

    def right_copy(c, i, end):
        to, at, direct, outer = route(c, i, 1, end)
        return outer, (
            direct, to, right_turned.at[lax.rem(z + i, 4)], right_in.at[at], send_r.at[2 * i + end], recv_r.at[at]
        )

    def right_arrived(at):
        pltpu.make_async_copy(right_in.at[at], right_in.at[at], recv_r.at[at]).wait()

    def right_hand(c, i):
        _, low = hands_on(c, i, 1)
        at = 2 * i + jnp.where(low, 0, 1)
        return at, hand_copy(low, right_in, at, send_g.at[i], recv_r.at[at])

    for first in (True, False):
        for i in (1, 3, 2, 0)[: 3 if first else 4]:
            for end in range(2):
                for c in range(2):
                    outer = route(c, i, 0, end)[3]
                    direct, *rest = left_copy(c, i, end)
                    launch(direct & (outer if first else jnp.logical_not(outer)), *rest)
    spread_right()

    pltpu.make_async_copy(col, col, recv_c).wait()
    for q in range(4):
        right_turned[q] = col[q].astype(F32).T.astype(BF16)

    def first_rights(c):
        for i in (1, 3, 2):
            for end in range(2):
                outer, (direct, *rest) = right_copy(c, i, end)
                launch(direct & outer, *rest)

    def other_rights(c, ranks):
        for i in ranks:
            for end in range(2):
                outer, (direct, *rest) = right_copy(c, i, end)
                launch(direct & jnp.logical_not(outer), *rest)

    def hand_rights(c):
        for i in (1, 3, 2):
            hands, _ = hands_on(c, i, 1)
            if hands is not None:

                @pl.when(hands)
                def _(i=i):
                    at, copy = right_hand(c, i)
                    right_arrived(at)
                    copy.start()

    on_core(first_rights)
    on_core(lambda c: other_rights(c, (1, 3)))
    for i in (1, 3, 2):
        for c in range(2):
            hands, _ = hands_on(c, i, 0)
            if hands is not None:

                @pl.when(hands)
                def _(c=c, i=i):
                    at, copy = left_hand(c, i)
                    left_arrived(c, at)
                    copy.start()

    left_out(0)

    def gate_rows(t, carry):
        rows = pl.ds(pl.multiple_of(t * 256, 256), 256)
        gate[rows, :] = jax.nn.sigmoid(
            jnp.dot(normed[rows, :].astype(BF16), w_gate[...], preferred_element_type=F32)
        )
        return carry

    lax.fori_loop(0, 8, gate_rows, 0)
    gain_col[...] = jnp.broadcast_to(out_gain[...], (128, 128)).T
    shift_col[...] = jnp.broadcast_to(out_shift[...], (128, 128)).T

    on_core(hand_rights)
    on_core(lambda c: other_rights(c, (2,)))
    left_out(1)
    left_out(3)
    on_core(lambda c: other_rights(c, (0,)))
    left_out(2)

    my_shift = my_q + 4 * core
    corner = lax.rem(z - my_shift + ROWS, ROWS) // 4
    my_left = corner // 2
    my_right = jnp.where(my_left == 0, corner, 3 - corner)
    left_base = lax.rem(my_shift - 2 + core + 8 * my_left + ROWS, ROWS)
    right_base = lax.rem(my_shift + 10 + core + 8 * my_right, ROWS)

    lanes_low = lax.broadcasted_iota(jnp.int32, (32, 128), 1) < 64

    def tile_send(i, h, a, half):
        row = lax.rem(left_base + lax.rem(10 - core - a // 2, 4) + 4 * (a % 2), ROWS)
        block = lax.rem(right_base + lax.rem(10 - core - i, 4) + 4 * h, ROWS)
        to = 2 * block + half
        src, dst = tiles.at[2 * i + h, a, half], gathered.at[4 * d + my_q]
        here = (row == z) & (to == d)

        @pl.when(jnp.logical_not(here))
        def _():
            pltpu.make_async_remote_copy(
                src_ref=src, dst_ref=dst, send_sem=send_t, recv_sem=recv_o, device_id=(row, to), device_id_type=MESH
            ).start()

        @pl.when(here)
        def _():
            pltpu.make_async_copy(src, dst, recv_o).start()

    def multiply(i, h):
        right = right_in[2 * i + h]
        for pair_index in range(4):
            both = jnp.concatenate([left_in[2 * pair_index], left_in[2 * pair_index + 1]], axis=1)
            grid = jnp.dot(right, both, preferred_element_type=F32)
            for side in range(2):
                m = grid[:, 128 * side : 128 * side + 128]
                kept = jnp.where(lanes_low, m[0:32], m[96:128])
                moved = jnp.where(lanes_low, m[32:64], m[64:96])
                tile = (kept + pltpu.roll(moved, 64, axis=1)).astype(BF16)
                a = 2 * pair_index + side
                tiles[2 * i + h, a] = tile.reshape(2, 16, 128)
                for half in range(2):
                    tile_send(i, h, a, half)

    pltpu.make_async_copy(left_in, left_in, recv_e).wait()

    for i in (1, 3, 2, 0):
        for h in range(2):
            waiting = jnp.array(True)
            for c in range(2):
                hands, low = hands_on(c, i, 1)
                if hands is not None:
                    handed = hands & (jnp.logical_not(low) if h else low)
                    waiting = waiting & jnp.logical_not((core == c) & handed)

            @pl.when(waiting)
            def _(i=i, h=h):
                right_arrived(2 * i + h)

        def half_rank(h, carry, i=i):
            multiply(i, h)
            return carry

        lax.fori_loop(0, 2, half_rank, 0)

    def gone(buffer, sem):
        pltpu.make_async_copy(buffer, buffer, sem).wait()

    gone(col.at[:, pl.ds(0, 31 * 16)], send_c)
    gone(left_in.at[:, pl.ds(0, 31 * 16)], send_e)
    for i in range(4):
        for c in range(2):
            for end in range(2):
                landed(*left_copy(c, i, end))
            hands, _ = hands_on(c, i, 0)
            if hands is not None:

                @pl.when(hands)
                def _(c=c, i=i):
                    left_hand(c, i)[1].wait_send()

    def rights_gone(c):
        for i in range(4):
            for end in range(2):
                landed(*right_copy(c, i, end)[1])
            hands, _ = hands_on(c, i, 1)
            if hands is not None:

                @pl.when(hands)
                def _(i=i):
                    right_hand(c, i)[1].wait_send()

    on_core(rights_gone)
    gone(gathered.at[pl.ds(0, 127)], send_t)

    @pl.when(lax.rem(d // 2 - right_base + 2 * ROWS, ROWS) >= 8)
    def _():
        gone(gathered.at[0], send_t)

    pltpu.make_async_copy(gathered, gathered, recv_o).wait()

    def total(t, carry):
        block = gathered[pl.ds(8 * t, 8)].astype(F32)
        return carry + jnp.sum(block, axis=0)

    centre = lax.fori_loop(0, 16, total, jnp.zeros((16, 128), F32)) * (1.0 / 128)

    def squares(t, carry):
        block = gathered[pl.ds(8 * t, 8)].astype(F32) - centre[None]
        return carry + jnp.sum(block * block, axis=0)

    second = lax.fori_loop(0, 16, squares, jnp.zeros((16, 128), F32)) * (1.0 / 128)
    scale = lax.rsqrt(second + NORM_EPS)

    def centre_rows(t, carry):
        block = (gathered[pl.ds(8 * t, 8)].astype(F32) - centre[None]) * scale[None]
        wide_out[pl.ds(pl.multiple_of(t * 128, 128), 128), :] = block.reshape(128, 128)
        return carry

    lax.fori_loop(0, 16, centre_rows, 0, unroll=2)

    def project(jj, carry):
        x = wide_out[pl.ds(jj, 128, stride=16), :] * gain_col[...] + shift_col[...]
        out = jnp.dot(x.T.astype(BF16), w_out[...], preferred_element_type=F32)
        for j2 in range(2):
            for s, b in enumerate(BLOCK_ORDER):
                rows = pl.ds(b * 512 + j2 * 16 + jj, 16, stride=32)
                gate[rows, :] = gate[rows, :] * out[64 * j2 + 16 * s : 64 * j2 + 16 * s + 16]
        return carry

    lax.fori_loop(0, 16, project, 0, unroll=4)
    update[...] = gate[...].astype(BF16)


def on_device(pair, pair_mask, norm_gain, norm_shift, w_in, out_gain, out_shift, w_out, w_gate):
    vmem = pl.BlockSpec(memory_space=pltpu.VMEM)
    dma = pltpu.SemaphoreType.DMA
    out = pl.pallas_call(
        body,
        out_shape=jax.ShapeDtypeStruct((2048, 128), BF16),
        in_specs=[pl.BlockSpec(memory_space=pl.ANY)] * 9,
        out_specs=vmem,
        scratch_shapes=[
            pltpu.VMEM((2048, 128), BF16),
            pltpu.VMEM((32, 64), jnp.int32),
            pltpu.VMEM((1, 128), F32),
            pltpu.VMEM((1, 128), F32),
            pltpu.VMEM((128, 512), BF16),
            pltpu.VMEM((1, 128), F32),
            pltpu.VMEM((1, 128), F32),
            pltpu.VMEM((128, 128), BF16),
            pltpu.VMEM((128, 128), BF16),
            dma((9,)),
            pltpu.VMEM((2048, 128), F32),
            pltpu.VMEM((2048, 128), F32),
            pltpu.VMEM((2048, 128), F32),
            pltpu.VMEM((512, 128), BF16),
            pltpu.VMEM((16, 128), F32),
            pltpu.VMEM((2, 4, 2, 16, 16, 128), BF16),
            pltpu.VMEM((8, 2, 16, 16, 128), BF16),
            pltpu.VMEM((4, 512, 128), BF16),
            pltpu.VMEM((4, 128, 512), BF16),
            pltpu.VMEM((8, 512, 128), BF16),
            pltpu.VMEM((8, 128, 512), BF16),
            pltpu.VMEM((8, 8, 2, 16, 128), BF16),
            pltpu.VMEM((128, 16, 128), BF16),
            pltpu.VMEM((2048, 128), F32),
            pltpu.VMEM((2048, 128), F32),
            pltpu.VMEM((128, 128), F32),
            pltpu.VMEM((128, 128), F32),
            dma, dma, dma((16,)), dma((16,)), dma((8,)),
            dma((8,)), dma((8,)), dma((4,)),
            dma, dma, dma, dma,
        ],
        compiler_params=pltpu.CompilerParams(
            collective_id=0, has_side_effects=True, vmem_limit_bytes=56 << 20
        ),
    )(
        pair.reshape(2048, 128), pair_mask.T, norm_gain.reshape(1, 128), norm_shift.reshape(1, 128), w_in,
        out_gain.reshape(1, 128), out_shift.reshape(1, 128), w_out, w_gate,
    )
    return out.reshape(64, 32, 128)


def solution(mesh):
    in_specs = (P("row", "col", None), P("row", "col"), P(), P(), P(), P(), P(), P(), P())
    out_specs = P("row", "col", None)
    return jax.shard_map(on_device, mesh=mesh, in_specs=in_specs, out_specs=out_specs, check_vma=False)
```
